32 devices in a mesh: ctx: 4 (over y, x), head: 4 (over z), pool: 2 (over core).
Axes of the slice: x: 2, y: 2, z: 4, core: 2. Of those that a mesh axis runs over, the one named last changes fastest.
Arguments:
- queries: bfloat16 [2, 512, 4096], P(None, ('ctx', 'pool'), 'head')
- stretch_keys: bfloat16 [2, 512, 512], P(None, ('ctx', 'pool'), 'head'), may hold values from -6 to 6
- stretch_values: bfloat16 [2, 512, 512], P(None, ('ctx', 'pool'), 'head'), may hold values from -6 to 6
- slot_pool_keys: bfloat16 [64, 64, 512], P(('ctx', 'head', 'pool')), may hold values from -6 to 6
- slot_pool_values: bfloat16 [64, 64, 512], P(('ctx', 'head', 'pool')), may hold values from -6 to 6
- prefix_lengths: int32 [2], replicated, may hold values from 512 to 2048
- page_slot_table: int32 [64], replicated, may hold values from 0 to 63, each once
- vertical: int32 [32, 16], replicated, may hold values from 0 to 31
- slash: int32 [32, 16], replicated, may hold values from 0 to 31
Outputs:
- attended: bfloat16 [2, 512, 4096], P(None, ('ctx', 'pool'), 'head')
The draws below stay inside these ranges and needn't reach their ends.
Inputs may be any that keep to these rules, and one draw needn't show every extreme that they name: `page_slot_table`: each pool slot is named exactly once; entry 32 * b + j is the slot of page j of prompt b.
All inputs are finite; a program needn't handle non-finite values.
Results may differ from the reference program's by a relative error of at most 0.0075.
Values may be sent and summed in bfloat16 or wider, within the bound.
No kernel may reach another device: no remote copies, remote signals or barrier semaphores. Data moves between devices by JAX's collectives and lax.ppermute only.
A program may use at most 128 MiB of HBM per device.

```python
import math
import jax
import jax.numpy as jnp
from jax import lax

HEAD_SIZE = 128
GROUP = 8
PAGE_TOKENS = 64
PROMPTS = 2
NV = 16
NS = 16
KEY_VALUE_HEADS = 4
HEADS = 32
SLOT_COUNT = 64
PAGES = 32
PREFIX = 2048
STRETCH = 512


def draw_queries(key, part):
    key = jax.random.fold_in(key, 11)
    first = jax.random.fold_in(key, 0)
    array_shape = (PROMPTS, STRETCH, HEADS * HEAD_SIZE)
    values = jax.random.truncated_normal(first, -6.0, 6.0, array_shape, jnp.float32)
    return values.astype(jnp.bfloat16)


def place_ends(values, own_key, least, top_value):
    index_at = [jax.random.randint(jax.random.fold_in(own_key, axis), (), 0, length) for axis, length in enumerate(values.shape)]
    widest = values.shape.index(max(values.shape))
    next_to = index_at[:widest] + [(index_at[widest] + 1) % values.shape[widest]] + index_at[widest + 1:]
    return values.at[tuple(index_at)].set(least).at[tuple(next_to)].set(top_value)


def shard_levels(own_key, shape, cuts, smallest, top_value):
    level = 1.0
    for position, parts in cuts:
        draws = jax.random.uniform(jax.random.fold_in(jax.random.fold_in(own_key, 6), position), (parts,), jnp.float32, smallest / len(cuts), top_value / len(cuts))
        level = level * jnp.repeat(jnp.exp(draws), shape[position] // parts).reshape((-1,) + (1,) * (len(shape) - 1 - position))
    return level


def normal_values(own_key, extent, width, reach, cuts=(), held_as=jnp.bfloat16):
    values = width * jax.random.normal(own_key, extent, jnp.float32)
    if cuts:
        values = values * shard_levels(own_key, extent, cuts, -0.22, 0.18)
    return jnp.clip(values, -reach, reach).astype(held_as)


def setup_inputs(seed: int = 0) -> dict:
    arg_keys = jax.random.split(jax.random.key(seed), 10)
    return {
        "queries": draw_queries(jax.random.fold_in(arg_keys[9], 71), 0),
        "stretch_keys": normal_values(arg_keys[1], (PROMPTS, STRETCH, KEY_VALUE_HEADS * HEAD_SIZE), 1.0, 6.0, ((1, 8), (2, 4))),
        "stretch_values": normal_values(arg_keys[2], (PROMPTS, STRETCH, KEY_VALUE_HEADS * HEAD_SIZE), 1.0, 6.0, ((1, 8), (2, 4))),
        "slot_pool_keys": normal_values(arg_keys[3], (SLOT_COUNT, PAGE_TOKENS, KEY_VALUE_HEADS * HEAD_SIZE), 1.0, 6.0, ((0, 32),)),
        "slot_pool_values": normal_values(arg_keys[4], (SLOT_COUNT, PAGE_TOKENS, KEY_VALUE_HEADS * HEAD_SIZE), 1.0, 6.0, ((0, 32),)),
        "prefix_lengths": jax.random.randint(arg_keys[5], (PROMPTS,), PREFIX // 4, PREFIX + 1).astype(jnp.int32),
        "page_slot_table": jax.random.permutation(arg_keys[6], SLOT_COUNT).astype(jnp.int32),
        "vertical": place_ends(jax.random.randint(arg_keys[7], (HEADS, NV), 0, PAGES), jax.random.fold_in(arg_keys[7], 1), 0, PAGES - 1).astype(jnp.int32),
        "slash": place_ends(jax.random.randint(arg_keys[8], (HEADS, NS), 0, PAGES), jax.random.fold_in(arg_keys[8], 1), 0, PAGES - 1).astype(jnp.int32),
    }


very_low = -1e+30

def reference(queries, stretch_keys, stretch_values, slot_pool_keys, slot_pool_values, prefix_lengths, page_slot_table, vertical, slash):
    scaling = 1.0 / math.sqrt(HEAD_SIZE)
    table = page_slot_table.reshape(PROMPTS, PAGES)
    prefix_keys = slot_pool_keys[table].reshape(PROMPTS, PREFIX, KEY_VALUE_HEADS * HEAD_SIZE)
    prefix_values = slot_pool_values[table].reshape(PROMPTS, PREFIX, KEY_VALUE_HEADS * HEAD_SIZE)
    all_keys = jnp.concatenate([prefix_keys, stretch_keys], axis=1)
    all_values = jnp.concatenate([prefix_values, stretch_values], axis=1)
    row_block = min(STRETCH, 256)
    blocks = STRETCH // row_block
    key_ids = jnp.arange(PREFIX + STRETCH, dtype=jnp.int32)
    page_ids = jnp.arange(PAGES, dtype=jnp.int32)

    def one_block(number):
        prompt = number // (KEY_VALUE_HEADS * blocks)
        group_id = number // blocks % KEY_VALUE_HEADS
        first_row = number % blocks * row_block
        zero = jnp.zeros((), jnp.int32)
        query_block = lax.dynamic_slice(queries, (prompt, first_row, group_id * GROUP * HEAD_SIZE), (1, row_block, GROUP * HEAD_SIZE))[0]
        query_block = query_block.reshape(row_block, GROUP, HEAD_SIZE)
        key_block = lax.dynamic_slice(all_keys, (prompt, zero, group_id * HEAD_SIZE), (1, PREFIX + STRETCH, HEAD_SIZE))[0]
        value_block = lax.dynamic_slice(all_values, (prompt, zero, group_id * HEAD_SIZE), (1, PREFIX + STRETCH, HEAD_SIZE))[0]
        scores = jnp.einsum('rgd,kd->grk', query_block.astype(jnp.float32), key_block.astype(jnp.float32)) * scaling
        prefix_len = prefix_lengths[prompt]
        row_ids = first_row + jnp.arange(row_block, dtype=jnp.int32)
        query_page = (prefix_len + row_ids) // PAGE_TOKENS
        vert_rows = lax.dynamic_slice_in_dim(vertical, group_id * GROUP, GROUP, 0)
        slash_rows = lax.dynamic_slice_in_dim(slash, group_id * GROUP, GROUP, 0)
        vert_hit = jnp.any(vert_rows[:, :, None] == page_ids[None, None, :], axis=1)
        distance = query_page[:, None] - page_ids[None, :]
        slash_hit = jnp.any(slash_rows[:, :, None, None] == distance[None, None], axis=1)
        chosen = vert_hit[:, None, :] | slash_hit
        chosen_keys = jnp.repeat(chosen, PAGE_TOKENS, axis=2)
        live_keys = key_ids[:PREFIX] < prefix_len
        prefix_ok = chosen_keys & live_keys[None, None, :]
        causal = key_ids[None, PREFIX:] - PREFIX <= row_ids[:, None]
        causal = jnp.broadcast_to(causal[None], (GROUP, row_block, STRETCH))
        allowed = jnp.concatenate([prefix_ok, causal], axis=2)
        highest = lax.optimization_barrier(jnp.max(jnp.where(allowed, scores, very_low), axis=-1, keepdims=True))
        weights = jnp.where(allowed, jnp.exp(scores - highest), 0.0)
        totals = lax.optimization_barrier(jnp.sum(weights, axis=-1))
        rounded = lax.optimization_barrier(weights.astype(jnp.bfloat16))
        numerator = jnp.einsum('grk,kd->grd', rounded.astype(jnp.float32), value_block.astype(jnp.float32))
        result = numerator / totals[..., None]
        return result.transpose(1, 0, 2).reshape(row_block, GROUP * HEAD_SIZE).astype(jnp.bfloat16)
    outputs = lax.map(one_block, jnp.arange(PROMPTS * KEY_VALUE_HEADS * blocks, dtype=jnp.int32))
    outputs = outputs.reshape(PROMPTS, KEY_VALUE_HEADS, blocks, row_block, GROUP * HEAD_SIZE)
    outputs = outputs.transpose(0, 2, 3, 1, 4).reshape(PROMPTS, STRETCH, KEY_VALUE_HEADS * GROUP * HEAD_SIZE)
    return outputs
```

```python
import math

import jax
import jax.numpy as jnp
from jax import lax
from jax.experimental import pallas as pl
from jax.experimental.pallas import tpu as pltpu
from jax.sharding import PartitionSpec as P

very_low = -1e30


def absorb(running, scores, allowed, values):
    highest, totals, numerator = running
    new_high = jnp.maximum(highest, jnp.max(jnp.where(allowed, scores, very_low), axis=-1))
    factor = jnp.exp(highest - new_high)
    weights = jnp.where(allowed, jnp.exp(scores - new_high[..., None]), 0.0)
    totals = totals * factor + jnp.sum(weights, axis=-1)
    numerator = numerator * factor[..., None] + jnp.einsum(
        "grk,kd->grd", weights.astype(jnp.bfloat16), values, preferred_element_type=jnp.float32
    )
    return (new_high, totals, numerator)


def body(
    queries,
    stretch_keys,
    stretch_values,
    slot_pool_keys,
    slot_pool_values,
    prefix_lengths,
    page_slot_table,
    vertical,
    slash,
):
    prompts, local_rows, row_width = queries.shape
    head_dim = stretch_keys.shape[2]
    group_size = row_width // head_dim
    page_len = slot_pool_keys.shape[1]
    owner_slots = slot_pool_keys.shape[0]
    slot_total = page_slot_table.shape[0]
    page_count = slot_total // prompts
    head_count = lax.axis_size("head")
    pool_count = lax.axis_size("pool")
    ctx_count = lax.axis_size("ctx")
    plane_size = ctx_count * pool_count
    ctx_index = lax.axis_index("ctx")
    pool_index = lax.axis_index("pool")
    head_index = lax.axis_index("head")
    plane_index = ctx_index * pool_count + pool_index
    stretch_len = plane_size * local_rows
    scaling = 1.0 / math.sqrt(head_dim)
    vert_rows = lax.dynamic_slice_in_dim(vertical, head_index * group_size, group_size, 0)
    slash_rows = lax.dynamic_slice_in_dim(slash, head_index * group_size, group_size, 0)
    page_ids = jnp.arange(page_count, dtype=jnp.int32)
    vert_hit = jnp.any(vert_rows[:, :, None] == page_ids[None, None, :], axis=1)
    row_ids = plane_index * local_rows + jnp.arange(local_rows, dtype=jnp.int32)
    page_keys, page_values = (
        lax.all_to_all(slot_pool_keys, "head", split_axis=2, concat_axis=0, tiled=True),
        lax.all_to_all(slot_pool_values, "head", split_axis=2, concat_axis=0, tiled=True),
    )
    held_slots = owner_slots * head_count
    empty_state = (
        jnp.full((group_size, local_rows), very_low, jnp.float32),
        jnp.zeros((group_size, local_rows), jnp.float32),
        jnp.zeros((group_size, local_rows, head_dim), jnp.float32),
    )
    plane_keys, plane_values = (
        lax.all_gather(page_keys, ("ctx", "pool"), axis=0, tiled=True),
        lax.all_gather(page_values, ("ctx", "pool"), axis=0, tiled=True),
    )
    owner_index = page_slot_table // owner_slots
    within = page_slot_table % owner_slots
    owner_pool = owner_index % pool_count
    owner_head = owner_index // pool_count % head_count
    owner_ctx = owner_index // (pool_count * head_count)
    location = (
        (owner_ctx * pool_count + owner_pool) * held_slots + owner_head * owner_slots + within
    )
    ordered_keys = jnp.take(plane_keys, location, axis=0).reshape(
        prompts, page_count * page_len, head_dim
    )
    ordered_values = jnp.take(plane_values, location, axis=0).reshape(
        prompts, page_count * page_len, head_dim
    )
    key_span = min(2048, page_count * page_len)
    states = []
    for prompt in range(prompts):
        prefix_len = prefix_lengths[prompt]
        query_page = (prefix_len + row_ids) // page_len
        query_block = queries[prompt].reshape(local_rows, group_size, head_dim)
        prompt_keys = ordered_keys[prompt]
        prompt_values = ordered_values[prompt]

        def prefix_step(block_index, running):
            first_key = block_index * key_span
            key_part = lax.dynamic_slice_in_dim(prompt_keys, first_key, key_span, 0)
            value_part = lax.dynamic_slice_in_dim(prompt_values, first_key, key_span, 0)
            key_ids = first_key + jnp.arange(key_span, dtype=jnp.int32)
            first_page = first_key // page_len
            page_part = lax.dynamic_slice_in_dim(vert_hit, first_page, key_span // page_len, 1)
            distance = (
                query_page[:, None]
                - (first_page + jnp.arange(key_span // page_len, dtype=jnp.int32))[None, :]
            )
            slash_hit = jnp.any(slash_rows[:, :, None, None] == distance[None, None], axis=1)
            chosen = page_part[:, None, :] | slash_hit
            allowed = jnp.repeat(chosen, page_len, axis=2) & (key_ids < prefix_len)[None, None, :]
            scores = (
                jnp.einsum("rgd,kd->grk", query_block, key_part, preferred_element_type=jnp.float32)
                * scaling
            )
            return absorb(running, scores, allowed, value_part)

        upper_bound = (prefix_len + key_span - 1) // key_span
        states.append(lax.fori_loop(0, upper_bound, prefix_step, empty_state))
    plane_stretch_keys, plane_stretch_values = (
        lax.all_gather(stretch_keys, ("ctx", "pool"), axis=1, tiled=True),
        lax.all_gather(stretch_values, ("ctx", "pool"), axis=1, tiled=True),
    )
    stretch_span = min(2048, stretch_len)
    outputs = []
    for prompt in range(prompts):
        query_block = queries[prompt].reshape(local_rows, group_size, head_dim)
        prompt_keys = plane_stretch_keys[prompt]
        prompt_values = plane_stretch_values[prompt]

        def stretch_step(block_index, running):
            first_key = block_index * stretch_span
            key_ids = first_key + jnp.arange(stretch_span, dtype=jnp.int32)
            allowed = jnp.broadcast_to(
                (key_ids[None, :] <= row_ids[:, None])[None], (group_size, local_rows, stretch_span)
            )
            scores = (
                jnp.einsum(
                    "rgd,kd->grk", query_block, prompt_keys, preferred_element_type=jnp.float32
                )
                * scaling
            )
            return absorb(running, scores, allowed, prompt_values)

        upper_bound = (plane_index * local_rows + local_rows - 1) // stretch_span + 1
        highest, totals, numerator = lax.fori_loop(0, upper_bound, stretch_step, states[prompt])
        result = numerator / totals[..., None]
        outputs.append(
            result.transpose(1, 0, 2).reshape(local_rows, row_width).astype(jnp.bfloat16)
        )
    return jnp.stack(outputs)


page_axes = ("ctx", "pool")
roles = 4
hide = -(2.0**126)
log2e = 1.4426950408889634


def split_kernel(
    pool_keys, pool_values, stretch_keys, stretch_values, first, second, third, early, sems
):
    head = lax.axis_index("head")
    copies = []

    def add(source, target):
        copy = pltpu.make_async_copy(source, target, sems.at[len(copies)])
        copy.start()
        copies.append(copy)

    for shift, target in ((3, third), (2, second), (1, first), (0, None)):
        columns = pl.ds(pl.multiple_of((head ^ shift) * 128, 128), 128)
        for which, pool in enumerate((pool_keys, pool_values)):
            place = early.at[2 + which] if target is None else target.at[which]
            add(pool.at[:, :, columns], place)
    add(stretch_keys, early.at[0])
    add(stretch_values, early.at[1])
    for copy in copies:
        copy.wait()


def split(pool_keys, pool_values, stretch_keys, stretch_values):
    piece = pltpu.VMEM((2, 2, 64, 128), jnp.bfloat16)
    bundle = pltpu.VMEM((4, 2, 64, 128), jnp.bfloat16)
    return pl.pallas_call(
        split_kernel,
        out_shape=(piece, piece, piece, bundle),
        in_specs=[pl.BlockSpec(memory_space=pl.ANY)] * 4,
        out_specs=[pl.BlockSpec(memory_space=pltpu.VMEM)] * 4,
        scratch_shapes=[pltpu.SemaphoreType.DMA((10,))],
        name="split",
    )(pool_keys, pool_values, stretch_keys, stretch_values)


def mask_kernel(lengths, queries, vertical, slash, wide_queries, key_tags):
    head = lax.axis_index("head")
    plane = lax.axis_index("ctx") * 2 + lax.axis_index("pool")
    first_row = plane * 64
    rows8 = pl.ds(pl.multiple_of(head * 8, 8), 8)
    vert_rows = vertical[rows8, :]
    slash_rows = slash[rows8, :]
    lane8 = lax.broadcasted_iota(jnp.int32, (8, 128), 1)
    lane = lax.broadcasted_iota(jnp.int32, (64, 128), 1)
    row = lax.broadcasted_iota(jnp.int32, (64, 128), 0)
    vert_hit = lane8 < 0
    for entry in range(16):
        vert_hit = vert_hit | (vert_rows[:, entry : entry + 1] == lane8)
    causal = jnp.where(lane - 64 <= row, 0.0, hide)
    for prompt in range(2):
        length = lengths[prompt]
        base_page = (length + first_row) // 64
        cut = (base_page + 1) * 64 - length - first_row
        tables = []
        for step in range(2):
            hit = vert_hit
            distance = base_page + step - lane8
            for entry in range(16):
                hit = hit | (slash_rows[:, entry : entry + 1] == distance)
            hit = hit & (lane8 * 64 < length)
            shown = (hit & (lane8 < 32)) | (lane8 > 33)
            tables.append(jnp.where(shown, 0.0, hide))
        for group in range(8):
            own = slice(group * 64, (group + 1) * 64)
            bias = jnp.where(
                row < cut, tables[0][group : group + 1, :], tables[1][group : group + 1, :]
            )
            bias = jnp.where(lane < 64, bias, causal)
            wide_queries[prompt, own, :128] = queries[prompt, :, group * 128 : (group + 1) * 128]
            wide_queries[prompt, own, 128:] = bias.astype(jnp.bfloat16)
        for page in range(32):
            tag = (lane == page) | ((lane == 32) & (row + page * 64 >= length))
            key_tags[prompt, page * 64 : (page + 1) * 64, :] = jnp.where(tag, 1.0, 0.0).astype(
                jnp.bfloat16
            )
        for page in range(8):
            diagonal = (lane - 64 == row) & (plane == page)
            tag = diagonal | ((lane == 33) & (plane < page))
            key_tags[prompt, 2048 + page * 64 : 2048 + (page + 1) * 64, :] = jnp.where(
                tag, 1.0, 0.0
            ).astype(jnp.bfloat16)


def mask(lengths, queries, vertical, slash):
    return pl.pallas_call(
        mask_kernel,
        out_shape=(
            pltpu.VMEM((2, 512, 256), jnp.bfloat16),
            pltpu.VMEM((2, 2560, 128), jnp.bfloat16),
        ),
        in_specs=[pl.BlockSpec(memory_space=pltpu.SMEM)]
        + [pl.BlockSpec(memory_space=pltpu.VMEM)] * 3,
        out_specs=[pl.BlockSpec(memory_space=pltpu.VMEM)] * 2,
        name="mask",
    )(lengths, queries, vertical, slash)


def attend_kernel(table, wide_queries, key_tags, *rest):
    early, late = rest[:8], rest[8:16]
    result, where_is, keys, values = rest[16:]
    ctx, head, pool = lax.axis_index("ctx"), lax.axis_index("head"), lax.axis_index("pool")

    def invert(index, carry):
        where_is[table[index]] = (index // 32) * 2560 + (index % 32) * 64
        return carry

    lax.fori_loop(0, 64, invert, 0)
    for other in range(2):
        from_pool = pool ^ other
        for role in range(roles):
            near = (0, 1 + from_pool, 2 - from_pool, 3)[role]
            from_ctx = ctx ^ near
            bundle, pieces = early[other * 4 + role], late[other * 4 + role]
            for prompt in range(2):
                start = pl.multiple_of(
                    prompt * 2560 + 2048 + (from_ctx * 2 + from_pool) * 64, 64
                )
                keys[pl.ds(start, 64), :] = bundle[0, prompt]
                values[pl.ds(start, 64), :] = bundle[1, prompt]
            for shift in range(4):
                first_slot = ((from_ctx * 4 + (head ^ shift)) * 2 + from_pool) * 2
                for within in range(2):
                    start = pl.multiple_of(where_is[first_slot + within], 64)
                    if shift == 0:
                        page_keys, page_values = bundle[2, within], bundle[3, within]
                    else:
                        page_keys = pieces[shift - 1, 0, within]
                        page_values = pieces[shift - 1, 1, within]
                    keys[pl.ds(start, 64), :] = page_keys
                    values[pl.ds(start, 64), :] = page_values
    scale = log2e / math.sqrt(128.0)
    ones = jnp.ones((2560, 128), jnp.bfloat16)
    for prompt in range(2):
        span = slice(prompt * 2560, (prompt + 1) * 2560)
        wide_keys = jnp.concatenate([keys[span, :], key_tags[prompt]], axis=1)
        wide_values = jnp.concatenate([values[span, :], ones], axis=1)
        for part in range(2):
            scores = lax.dot_general(
                wide_queries[prompt, part * 256 : (part + 1) * 256, :],
                wide_keys,
                (((1,), (1,)), ((), ())),
                preferred_element_type=jnp.float32,
            )
            highest = jnp.max(scores, axis=1, keepdims=True)
            weights = jnp.exp2((scores - highest) * scale).astype(jnp.bfloat16)
            sums = jnp.dot(weights, wide_values, preferred_element_type=jnp.float32)
            attended = (sums[:, :128] / sums[:, 128:]).astype(jnp.bfloat16)
            for group in range(4):
                column = (part * 4 + group) * 128
                result[prompt, :, column : column + 128] = attended[
                    group * 64 : (group + 1) * 64, :
                ]


def attend(table, wide_queries, key_tags, early, late):
    vmem = pl.BlockSpec(memory_space=pltpu.VMEM)
    return pl.pallas_call(
        attend_kernel,
        out_shape=jax.ShapeDtypeStruct((2, 64, 1024), jnp.bfloat16),
        in_specs=[pl.BlockSpec(memory_space=pltpu.SMEM)] + [vmem] * 18,
        out_specs=vmem,
        scratch_shapes=[
            pltpu.SMEM((64,), jnp.int32),
            pltpu.VMEM((5120, 128), jnp.bfloat16),
            pltpu.VMEM((5120, 128), jnp.bfloat16),
        ],
        compiler_params=pltpu.CompilerParams(vmem_limit_bytes=40 * 2**20),
        name="attend",
    )(table, wide_queries, key_tags, *early, *late)


def to_first(value):
    pairs = [(2 * c + p, 2 * (c ^ (1 + p)) + p) for c in range(4) for p in range(2)]
    return lax.ppermute(value, page_axes, pairs)


def to_second(value):
    pairs = [(2 * c + p, 2 * (c ^ (2 - p)) + p) for c in range(4) for p in range(2)]
    return lax.ppermute(value, page_axes, pairs)


def to_sibling(value):
    return lax.ppermute(value, "pool", [(0, 1), (1, 0)])


def spread(value):
    by_first = to_first(value)
    by_second = to_second(value)
    by_both = to_second(by_first)
    return [value, by_first, by_second, by_both]


def with_sibling(mine):
    return mine + [to_sibling(one) for one in mine]


def small_body(
    queries,
    stretch_keys,
    stretch_values,
    slot_pool_keys,
    slot_pool_values,
    prefix_lengths,
    page_slot_table,
    vertical,
    slash,
):
    first, second, third, bundle = split(
        slot_pool_keys, slot_pool_values, stretch_keys, stretch_values
    )
    arrived = [
        lax.ppermute(piece, "head", [(z, z ^ shift) for z in range(4)])
        for shift, piece in ((3, third), (2, second), (1, first))
    ]
    arrived.reverse()
    wide_queries, key_tags = mask(prefix_lengths, queries, vertical, slash)
    by_first, by_second = to_first(bundle), to_second(bundle)
    arrived, by_first, by_second, wide_queries, key_tags = lax.optimization_barrier(
        (arrived, by_first, by_second, wide_queries, key_tags)
    )
    early = with_sibling([bundle, by_first, by_second, to_second(by_first)])
    late = with_sibling(spread(jnp.stack(arrived)))
    return attend(page_slot_table, wide_queries, key_tags, early, late)


def solution(mesh):
    small = tuple(mesh.shape[axis] for axis in ("ctx", "head", "pool")) == (4, 4, 2)
    in_specs = (
        P(None, ("ctx", "pool"), "head"),
        P(None, ("ctx", "pool"), "head"),
        P(None, ("ctx", "pool"), "head"),
        P(("ctx", "head", "pool"), None, None),
        P(("ctx", "head", "pool"), None, None),
        P(),
        P(),
        P(),
        P(),
    )
    out_specs = P(None, ("ctx", "pool"), "head")
    return jax.shard_map(
        small_body if small else body,
        mesh=mesh,
        in_specs=in_specs,
        out_specs=out_specs,
        check_vma=False,
    )
```

```python
import math

import jax
import jax.numpy as jnp
from jax import lax
from jax.experimental import pallas as pl
from jax.experimental.pallas import tpu as pltpu
from jax.sharding import PartitionSpec as P

very_low = -1e30


def absorb(running, scores, allowed, values):
    highest, totals, numerator = running
    new_high = jnp.maximum(highest, jnp.max(jnp.where(allowed, scores, very_low), axis=-1))
    factor = jnp.exp(highest - new_high)
    weights = jnp.where(allowed, jnp.exp(scores - new_high[..., None]), 0.0)
    totals = totals * factor + jnp.sum(weights, axis=-1)
    numerator = numerator * factor[..., None] + jnp.einsum(
        "grk,kd->grd", weights.astype(jnp.bfloat16), values, preferred_element_type=jnp.float32
    )
    return (new_high, totals, numerator)


def body(
    queries,
    stretch_keys,
    stretch_values,
    slot_pool_keys,
    slot_pool_values,
    prefix_lengths,
    page_slot_table,
    vertical,
    slash,
):
    prompts, local_rows, row_width = queries.shape
    head_dim = stretch_keys.shape[2]
    group_size = row_width // head_dim
    page_len = slot_pool_keys.shape[1]
    owner_slots = slot_pool_keys.shape[0]
    slot_total = page_slot_table.shape[0]
    page_count = slot_total // prompts
    head_count = lax.axis_size("head")
    pool_count = lax.axis_size("pool")
    ctx_count = lax.axis_size("ctx")
    plane_size = ctx_count * pool_count
    ctx_index = lax.axis_index("ctx")
    pool_index = lax.axis_index("pool")
    head_index = lax.axis_index("head")
    plane_index = ctx_index * pool_count + pool_index
    stretch_len = plane_size * local_rows
    scaling = 1.0 / math.sqrt(head_dim)
    vert_rows = lax.dynamic_slice_in_dim(vertical, head_index * group_size, group_size, 0)
    slash_rows = lax.dynamic_slice_in_dim(slash, head_index * group_size, group_size, 0)
    page_ids = jnp.arange(page_count, dtype=jnp.int32)
    vert_hit = jnp.any(vert_rows[:, :, None] == page_ids[None, None, :], axis=1)
    row_ids = plane_index * local_rows + jnp.arange(local_rows, dtype=jnp.int32)
    page_keys, page_values = (
        lax.all_to_all(slot_pool_keys, "head", split_axis=2, concat_axis=0, tiled=True),
        lax.all_to_all(slot_pool_values, "head", split_axis=2, concat_axis=0, tiled=True),
    )
    held_slots = owner_slots * head_count
    empty_state = (
        jnp.full((group_size, local_rows), very_low, jnp.float32),
        jnp.zeros((group_size, local_rows), jnp.float32),
        jnp.zeros((group_size, local_rows, head_dim), jnp.float32),
    )
    plane_keys, plane_values = (
        lax.all_gather(page_keys, ("ctx", "pool"), axis=0, tiled=True),
        lax.all_gather(page_values, ("ctx", "pool"), axis=0, tiled=True),
    )
    owner_index = page_slot_table // owner_slots
    within = page_slot_table % owner_slots
    owner_pool = owner_index % pool_count
    owner_head = owner_index // pool_count % head_count
    owner_ctx = owner_index // (pool_count * head_count)
    location = (
        (owner_ctx * pool_count + owner_pool) * held_slots + owner_head * owner_slots + within
    )
    ordered_keys = jnp.take(plane_keys, location, axis=0).reshape(
        prompts, page_count * page_len, head_dim
    )
    ordered_values = jnp.take(plane_values, location, axis=0).reshape(
        prompts, page_count * page_len, head_dim
    )
    key_span = min(2048, page_count * page_len)
    states = []
    for prompt in range(prompts):
        prefix_len = prefix_lengths[prompt]
        query_page = (prefix_len + row_ids) // page_len
        query_block = queries[prompt].reshape(local_rows, group_size, head_dim)
        prompt_keys = ordered_keys[prompt]
        prompt_values = ordered_values[prompt]

        def prefix_step(block_index, running):
            first_key = block_index * key_span
            key_part = lax.dynamic_slice_in_dim(prompt_keys, first_key, key_span, 0)
            value_part = lax.dynamic_slice_in_dim(prompt_values, first_key, key_span, 0)
            key_ids = first_key + jnp.arange(key_span, dtype=jnp.int32)
            first_page = first_key // page_len
            page_part = lax.dynamic_slice_in_dim(vert_hit, first_page, key_span // page_len, 1)
            distance = (
                query_page[:, None]
                - (first_page + jnp.arange(key_span // page_len, dtype=jnp.int32))[None, :]
            )
            slash_hit = jnp.any(slash_rows[:, :, None, None] == distance[None, None], axis=1)
            chosen = page_part[:, None, :] | slash_hit
            allowed = jnp.repeat(chosen, page_len, axis=2) & (key_ids < prefix_len)[None, None, :]
            scores = (
                jnp.einsum("rgd,kd->grk", query_block, key_part, preferred_element_type=jnp.float32)
                * scaling
            )
            return absorb(running, scores, allowed, value_part)

        upper_bound = (prefix_len + key_span - 1) // key_span
        states.append(lax.fori_loop(0, upper_bound, prefix_step, empty_state))
    plane_stretch_keys, plane_stretch_values = (
        lax.all_gather(stretch_keys, ("ctx", "pool"), axis=1, tiled=True),
        lax.all_gather(stretch_values, ("ctx", "pool"), axis=1, tiled=True),
    )
    stretch_span = min(2048, stretch_len)
    outputs = []
    for prompt in range(prompts):
        query_block = queries[prompt].reshape(local_rows, group_size, head_dim)
        prompt_keys = plane_stretch_keys[prompt]
        prompt_values = plane_stretch_values[prompt]

        def stretch_step(block_index, running):
            first_key = block_index * stretch_span
            key_ids = first_key + jnp.arange(stretch_span, dtype=jnp.int32)
            allowed = jnp.broadcast_to(
                (key_ids[None, :] <= row_ids[:, None])[None], (group_size, local_rows, stretch_span)
            )
            scores = (
                jnp.einsum(
                    "rgd,kd->grk", query_block, prompt_keys, preferred_element_type=jnp.float32
                )
                * scaling
            )
            return absorb(running, scores, allowed, prompt_values)

        upper_bound = (plane_index * local_rows + local_rows - 1) // stretch_span + 1
        highest, totals, numerator = lax.fori_loop(0, upper_bound, stretch_step, states[prompt])
        result = numerator / totals[..., None]
        outputs.append(
            result.transpose(1, 0, 2).reshape(local_rows, row_width).astype(jnp.bfloat16)
        )
    return jnp.stack(outputs)


page_axes = ("ctx", "pool")
hide = -(2.0**126)
scale = 1.4426950408889634 / math.sqrt(128.0)
join_flops = 6 * 10**9
mask_flops = 0
vmem = pl.BlockSpec(memory_space=pltpu.VMEM)
smem = pl.BlockSpec(memory_space=pltpu.SMEM)


def split_kernel(
    pool_keys, pool_values, stretch_keys, stretch_values, first, second, third, early, sems
):
    head = lax.axis_index("head")
    copies = []

    def add(source, target):
        copy = pltpu.make_async_copy(source, target, sems.at[len(copies)])
        copy.start()
        copies.append(copy)

    for shift, target in ((3, third), (2, second), (1, first), (0, None)):
        columns = pl.ds(pl.multiple_of((head ^ shift) * 128, 128), 128)
        for which, pool in enumerate((pool_keys, pool_values)):
            place = early.at[2 + which] if target is None else target.at[which]
            add(pool.at[:, :, columns], place)
    add(stretch_keys, early.at[0])
    add(stretch_values, early.at[1])
    for copy in copies:
        copy.wait()


def split(pool_keys, pool_values, stretch_keys, stretch_values):
    piece = pltpu.VMEM((2, 2, 64, 128), jnp.bfloat16)
    bundle = pltpu.VMEM((6, 2, 64, 128), jnp.bfloat16)
    return pl.pallas_call(
        split_kernel,
        out_shape=(piece, piece, piece, bundle),
        in_specs=[pl.BlockSpec(memory_space=pltpu.HBM)] * 4,
        out_specs=[vmem] * 4,
        scratch_shapes=[pltpu.SemaphoreType.DMA((10,))],
        name="split",
    )(pool_keys, pool_values, stretch_keys, stretch_values)


def widen_kernel(bundle, piece, wide):
    wide[4:] = piece[...]


def widen(bundle, piece):
    return pl.pallas_call(
        widen_kernel,
        out_shape=pltpu.VMEM((6, 2, 64, 128), jnp.bfloat16),
        in_specs=[vmem] * 2,
        out_specs=vmem,
        input_output_aliases={0: 0},
        compiler_params=pltpu.CompilerParams(vmem_limit_bytes=4 * 2**20),
        cost_estimate=pl.CostEstimate(flops=0, bytes_accessed=1000, transcendentals=0),
        name="widen",
    )(bundle, piece)


def join_kernel(second, third, joined):
    for index, piece in enumerate((second, third)):
        for which in range(2):
            for within in range(2):
                start = index * 128 + within * 64
                joined[which, start : start + 64, :] = piece[which, within]


def join(second, third):
    return pl.pallas_call(
        join_kernel,
        out_shape=pltpu.VMEM((2, 256, 128), jnp.bfloat16),
        in_specs=[vmem] * 2,
        out_specs=vmem,
        compiler_params=pltpu.CompilerParams(vmem_limit_bytes=4 * 2**20),
        cost_estimate=pl.CostEstimate(
            flops=join_flops, bytes_accessed=400000, transcendentals=0
        ),
        name="join",
    )(second, third)


def mask_kernel(
    lengths_in,
    table_in,
    queries_in,
    vertical_in,
    slash_in,
    wide_queries,
    key_tags,
    meta,
    lengths,
    table,
    queries,
    vertical,
    slash,
    sems,
):
    pairs = (
        (table_in, table),
        (lengths_in, lengths),
        (vertical_in, vertical),
        (slash_in, slash),
        (queries_in, queries),
    )
    copies = []
    for index, (source, target) in enumerate(pairs):
        copies.append(pltpu.make_async_copy(source, target, sems.at[index]))
        copies[-1].start()
    head = lax.axis_index("head")
    plane = lax.axis_index("ctx") * 2 + lax.axis_index("pool")
    first_row = plane * 64
    lane8 = lax.broadcasted_iota(jnp.int32, (8, 128), 1)
    lane = lax.broadcasted_iota(jnp.int32, (64, 128), 1)
    row = lax.broadcasted_iota(jnp.int32, (64, 128), 0)
    causal = jnp.where(lane - 64 <= row, 0.0, hide)
    own_heads = lax.broadcasted_iota(jnp.int32, (8, 32), 0) + head * 8
    pick = (own_heads == lax.broadcasted_iota(jnp.int32, (8, 32), 1)).astype(jnp.float32)
    for page in range(8):
        diagonal = (lane - 64 == row) & (plane == page)
        tag = diagonal | (((lane == 0) | (lane == 32)) & (plane < page))
        start = 4096 + page * 64
        key_tags[start : start + 64, :] = jnp.where(tag, 1.0, 0.0).astype(jnp.bfloat16)
    for copy in copies:
        copy.wait()
    for index in range(64):
        meta[table[index]] = index * 64
    for prompt in range(2):
        meta[64 + prompt] = lengths[prompt]

    def own(entries):
        picked = lax.dot_general(
            pick,
            entries[...].astype(jnp.float32),
            (((1,), (1,)), ((), ())),
            preferred_element_type=jnp.float32,
        )
        return (picked + 0.5).astype(jnp.int32)

    vert_rows, slash_rows = own(vertical), own(slash)
    page8 = lane8 % 32
    vert_hit = lane8 < 0
    for entry in range(16):
        vert_hit = vert_hit | (vert_rows[:, entry : entry + 1] == page8)
    for prompt in range(2):
        length = lengths[prompt]
        base_page = (length + first_row) // 64
        cut = (base_page + 1) * 64 - length - first_row
        tables = []
        for step in range(2):
            hit = vert_hit
            distance = base_page + step - page8
            for entry in range(16):
                hit = hit | (slash_rows[:, entry : entry + 1] == distance)
            shown = hit & (page8 * 64 < length) & (lane8 // 32 == prompt)
            tables.append(jnp.where(shown, 0.0, hide))
        for group in range(8):
            rows = slice(group * 64, (group + 1) * 64)
            bias = jnp.where(
                row < cut, tables[0][group : group + 1, :], tables[1][group : group + 1, :]
            )
            bias = jnp.where(lane < 64, bias, causal)
            wide_queries[prompt, rows, :128] = queries[prompt, :, group * 128 : (group + 1) * 128]
            wide_queries[prompt, rows, 128:] = bias.astype(jnp.bfloat16)
        for page in range(32):
            live = row + page * 64 < length
            tag = (live & (lane == prompt * 32 + page)) | (
                ~live & ((lane == 0) | (lane == 32))
            )
            start = prompt * 2048 + page * 64
            key_tags[start : start + 64, :] = jnp.where(tag, 1.0, 0.0).astype(jnp.bfloat16)


def mask(lengths, table, queries, vertical, slash):
    return pl.pallas_call(
        mask_kernel,
        out_shape=(
            pltpu.VMEM((2, 512, 256), jnp.bfloat16),
            pltpu.VMEM((4608, 128), jnp.bfloat16),
            pltpu.SMEM((72,), jnp.int32),
        ),
        in_specs=[pl.BlockSpec(memory_space=pltpu.HBM)] * 5,
        out_specs=[vmem] * 2 + [smem],
        scratch_shapes=[
            pltpu.SMEM((2,), jnp.int32),
            pltpu.SMEM((64,), jnp.int32),
            pltpu.VMEM((2, 64, 1024), jnp.bfloat16),
            pltpu.VMEM((16, 32), jnp.int32),
            pltpu.VMEM((16, 32), jnp.int32),
            pltpu.SemaphoreType.DMA((5,)),
        ],
        cost_estimate=pl.CostEstimate(
            flops=mask_flops, bytes_accessed=1000, transcendentals=0
        ),
        name="mask",
    )(lengths, table, queries, vertical, slash)


def origin(other, role):
    from_pool = lax.axis_index("pool") ^ other
    return lax.axis_index("ctx") ^ (0, 1 + from_pool, 2 - from_pool, 3)[role], from_pool


def tags_at(meta, key_tags, slot):
    return key_tags[pl.ds(pl.multiple_of(meta[slot], 64), 64), :]


def bundle_pages(meta, key_tags, bundle, other, role):
    from_ctx, from_pool = origin(other, role)
    pages = []
    for shift in range(2):
        slot = ((from_ctx * 4 + (lax.axis_index("head") ^ shift)) * 2 + from_pool) * 2
        for within in range(2):
            tags = tags_at(meta, key_tags, slot + within)
            pages.append((bundle[2 + 2 * shift, within], tags, bundle[3 + 2 * shift, within]))
    return pages


def bundle_stretch(key_tags, bundle, other, role, prompt):
    from_ctx, from_pool = origin(other, role)
    start = pl.multiple_of(4096 + (from_ctx * 2 + from_pool) * 64, 64)
    return [(bundle[0, prompt], key_tags[pl.ds(start, 64), :], bundle[1, prompt])]


def joined_pages(meta, key_tags, pieces, other, role):
    from_ctx, from_pool = origin(other, role)
    pages = []
    for shift in range(2, 4):
        slot = ((from_ctx * 4 + (lax.axis_index("head") ^ shift)) * 2 + from_pool) * 2
        for within in range(2):
            place = slice((shift - 2) * 128 + within * 64, (shift - 2) * 128 + within * 64 + 64)
            tags = tags_at(meta, key_tags, slot + within)
            pages.append((pieces[0, place, :], tags, pieces[1, place, :]))
    return pages


def stack(pages):
    keys = jnp.concatenate([page[0] for page in pages], axis=0)
    tags = jnp.concatenate([page[1] for page in pages], axis=0)
    values = jnp.concatenate([page[2] for page in pages], axis=0)
    ones = jnp.ones(values.shape, jnp.bfloat16)
    return jnp.concatenate([keys, tags], axis=1), jnp.concatenate([values, ones], axis=1)


def absorb_pages(wide_queries, shared, own, state, scores):
    shared_keys, shared_values = stack(shared)
    width = shared_keys.shape[0]
    own = [stack(pages) if pages else None for pages in own]
    highs, results = [], []
    for prompt in range(2):
        high = None
        for start, pair in ((0, (shared_keys,)), (width, own[prompt])):
            if pair is None:
                continue
            found = lax.dot_general(
                wide_queries[prompt],
                pair[0],
                (((1,), (1,)), ((), ())),
                preferred_element_type=jnp.float32,
            )
            scores[prompt, :, start : start + found.shape[1]] = found
            for column in range(0, found.shape[1], 128):
                part = found[:, column : column + 128]
                high = part if high is None else jnp.maximum(high, part)
        if state is not None:
            high = jnp.maximum(high, state[0][prompt])
        highs.append(jnp.max(high, axis=1, keepdims=True))
    for prompt in range(2):
        highest = highs[prompt]
        weights = jnp.exp2((scores[prompt] - highest) * scale).astype(jnp.bfloat16)
        sums = jnp.dot(
            weights[:, :width], shared_values, preferred_element_type=jnp.float32
        )
        if own[prompt] is not None:
            sums += jnp.dot(
                weights[:, width:], own[prompt][1], preferred_element_type=jnp.float32
            )
        numerator, totals = sums[:, :128], sums[:, 128:]
        if state is not None:
            factor = jnp.exp2((state[0][prompt] - highest) * scale)
            numerator = numerator + state[1][prompt, :, :128] * factor
            totals = totals + state[1][prompt, :, 128:] * factor
        results.append((highest, numerator, totals))
    return results


def keep(results, high_out, sums_out):
    for prompt, (highest, numerator, totals) in enumerate(results):
        high_out[prompt] = jnp.broadcast_to(highest, (512, 128))
        sums_out[prompt, :, :128] = numerator
        sums_out[prompt, :, 128:] = totals


def open_kernel(meta, wide_queries, key_tags, *rest):
    bundles, pieces = rest[:6], rest[6:8]
    high_out, sums_out, scores = rest[8:]
    shared, own = [], ([], [])
    for other in range(2):
        for role in range(3):
            bundle = bundles[other * 3 + role]
            shared += bundle_pages(meta, key_tags, bundle, other, role)
            for prompt in range(2):
                own[prompt].extend(bundle_stretch(key_tags, bundle, other, role, prompt))
        shared += joined_pages(meta, key_tags, pieces[other], other, 0)
    keep(absorb_pages(wide_queries, shared, own, None, scores), high_out, sums_out)


def middle_kernel(meta, wide_queries, key_tags, before, given, *rest):
    bundles, pieces = rest[:2], rest[2:6]
    high_out, sums_out, scores = rest[6:]
    shared, own = [], ([], [])
    for other in range(2):
        shared += bundle_pages(meta, key_tags, bundles[other], other, 3)
        for prompt in range(2):
            own[prompt].extend(bundle_stretch(key_tags, bundles[other], other, 3, prompt))
        for role in range(2):
            shared += joined_pages(meta, key_tags, pieces[other * 2 + role], other, 1 + role)
    keep(absorb_pages(wide_queries, shared, own, (before, given), scores), high_out, sums_out)


def close_kernel(meta, wide_queries, key_tags, before, given, mine, theirs, result, scores):
    shared = joined_pages(meta, key_tags, mine, 0, 3) + joined_pages(meta, key_tags, theirs, 1, 3)
    results = absorb_pages(wide_queries, shared, ([], []), (before, given), scores)
    for prompt, (_, numerator, totals) in enumerate(results):
        attended = (numerator / totals).astype(jnp.bfloat16)
        for group in range(8):
            rows = slice(group * 64, (group + 1) * 64)
            result[prompt, :, group * 128 : (group + 1) * 128] = attended[rows, :]


def call(kernel, name, out_shape, keys, *operands):
    single = not isinstance(out_shape, tuple)
    return pl.pallas_call(
        kernel,
        out_shape=out_shape,
        in_specs=[smem] + [vmem] * (len(operands) - 1),
        out_specs=vmem if single else (vmem,) * len(out_shape),
        scratch_shapes=[pltpu.VMEM((2, 512, keys), jnp.float32)],
        compiler_params=pltpu.CompilerParams(vmem_limit_bytes=40 * 2**20),
        cost_estimate=pl.CostEstimate(flops=0, bytes_accessed=1000, transcendentals=0),
        name=name,
    )(*operands)


def running():
    return (pltpu.VMEM((2, 512, 128), jnp.float32), pltpu.VMEM((2, 512, 256), jnp.float32))


def open_stage(meta, wide_queries, key_tags, bundles, pieces):
    return call(
        open_kernel, "open", running(), 38 * 64, meta, wide_queries, key_tags, *bundles, *pieces
    )


def middle_stage(meta, wide_queries, key_tags, state, bundles, pieces):
    return call(
        middle_kernel, "middle", running(), 26 * 64,
        meta, wide_queries, key_tags, *state, *bundles, *pieces,
    )


def close_stage(meta, wide_queries, key_tags, state, mine, theirs):
    return call(
        close_kernel, "close", jax.ShapeDtypeStruct((2, 64, 1024), jnp.bfloat16), 8 * 64,
        meta, wide_queries, key_tags, *state, mine, theirs,
    )


def to_first(value):
    pairs = [(2 * c + p, 2 * (c ^ (1 + p)) + p) for c in range(4) for p in range(2)]
    return lax.ppermute(value, page_axes, pairs)


def to_second(value):
    pairs = [(2 * c + p, 2 * (c ^ (2 - p)) + p) for c in range(4) for p in range(2)]
    return lax.ppermute(value, page_axes, pairs)


def to_sibling(value):
    return lax.ppermute(value, "pool", [(0, 1), (1, 0)])


def small_body(
    queries,
    stretch_keys,
    stretch_values,
    slot_pool_keys,
    slot_pool_values,
    prefix_lengths,
    page_slot_table,
    vertical,
    slash,
):
    first, second, third, bundle = split(
        slot_pool_keys, slot_pool_values, stretch_keys, stretch_values
    )
    third, second, first = (
        lax.ppermute(piece, "head", [(z, z ^ shift) for z in range(4)])
        for shift, piece in ((3, third), (2, second), (1, first))
    )
    joined = join(second, third)
    bundle = widen(bundle, first)
    bundle, lengths = lax.optimization_barrier((bundle, prefix_lengths))
    by_first, by_second = to_first(bundle), to_second(bundle)
    masks = mask(lengths, page_slot_table, queries, vertical.T, slash.T)
    by_first, by_second, joined, masks = lax.optimization_barrier(
        (by_first, by_second, joined, masks)
    )
    wide_queries, key_tags, meta = masks
    late_first, late_second = to_first(joined), to_second(joined)
    by_both = to_second(by_first)
    early = [bundle, by_first, by_second]
    early += [to_sibling(one) for one in early]
    state = open_stage(meta, wide_queries, key_tags, early, [joined, to_sibling(joined)])
    late_first, late_second, by_both, state = lax.optimization_barrier(
        (late_first, late_second, by_both, state)
    )
    late_both = to_second(late_first)
    late = [late_first, late_second]
    late += [to_sibling(one) for one in late]
    state = middle_stage(
        meta, wide_queries, key_tags, state, [by_both, to_sibling(by_both)], late
    )
    state, late_both = lax.optimization_barrier((state, late_both))
    return close_stage(
        meta, wide_queries, key_tags, state, late_both, to_sibling(late_both)
    )


def solution(mesh):
    small = tuple(mesh.shape[axis] for axis in ("ctx", "head", "pool")) == (4, 4, 2)
    in_specs = (
        P(None, ("ctx", "pool"), "head"),
        P(None, ("ctx", "pool"), "head"),
        P(None, ("ctx", "pool"), "head"),
        P(("ctx", "head", "pool"), None, None),
        P(("ctx", "head", "pool"), None, None),
        P(),
        P(),
        P(),
        P(),
    )
    out_specs = P(None, ("ctx", "pool"), "head")
    return jax.shard_map(
        small_body if small else body,
        mesh=mesh,
        in_specs=in_specs,
        out_specs=out_specs,
        check_vma=False,
    )
```

```python
import math

import jax
import jax.numpy as jnp
from jax import lax
from jax.experimental import pallas as pl
from jax.experimental.pallas import tpu as pltpu
from jax.sharding import PartitionSpec as P

very_low = -1e30


def absorb(running, scores, allowed, values):
    highest, totals, numerator = running
    new_high = jnp.maximum(highest, jnp.max(jnp.where(allowed, scores, very_low), axis=-1))
    factor = jnp.exp(highest - new_high)
    weights = jnp.where(allowed, jnp.exp(scores - new_high[..., None]), 0.0)
    totals = totals * factor + jnp.sum(weights, axis=-1)
    numerator = numerator * factor[..., None] + jnp.einsum(
        "grk,kd->grd", weights.astype(jnp.bfloat16), values, preferred_element_type=jnp.float32
    )
    return (new_high, totals, numerator)


def body(
    queries,
    stretch_keys,
    stretch_values,
    slot_pool_keys,
    slot_pool_values,
    prefix_lengths,
    page_slot_table,
    vertical,
    slash,
):
    prompts, local_rows, row_width = queries.shape
    head_dim = stretch_keys.shape[2]
    group_size = row_width // head_dim
    page_len = slot_pool_keys.shape[1]
    owner_slots = slot_pool_keys.shape[0]
    slot_total = page_slot_table.shape[0]
    page_count = slot_total // prompts
    head_count = lax.axis_size("head")
    pool_count = lax.axis_size("pool")
    ctx_count = lax.axis_size("ctx")
    plane_size = ctx_count * pool_count
    ctx_index = lax.axis_index("ctx")
    pool_index = lax.axis_index("pool")
    head_index = lax.axis_index("head")
    plane_index = ctx_index * pool_count + pool_index
    stretch_len = plane_size * local_rows
    scaling = 1.0 / math.sqrt(head_dim)
    vert_rows = lax.dynamic_slice_in_dim(vertical, head_index * group_size, group_size, 0)
    slash_rows = lax.dynamic_slice_in_dim(slash, head_index * group_size, group_size, 0)
    page_ids = jnp.arange(page_count, dtype=jnp.int32)
    vert_hit = jnp.any(vert_rows[:, :, None] == page_ids[None, None, :], axis=1)
    row_ids = plane_index * local_rows + jnp.arange(local_rows, dtype=jnp.int32)
    page_keys, page_values = (
        lax.all_to_all(slot_pool_keys, "head", split_axis=2, concat_axis=0, tiled=True),
        lax.all_to_all(slot_pool_values, "head", split_axis=2, concat_axis=0, tiled=True),
    )
    held_slots = owner_slots * head_count
    empty_state = (
        jnp.full((group_size, local_rows), very_low, jnp.float32),
        jnp.zeros((group_size, local_rows), jnp.float32),
        jnp.zeros((group_size, local_rows, head_dim), jnp.float32),
    )
    plane_keys, plane_values = (
        lax.all_gather(page_keys, ("ctx", "pool"), axis=0, tiled=True),
        lax.all_gather(page_values, ("ctx", "pool"), axis=0, tiled=True),
    )
    owner_index = page_slot_table // owner_slots
    within = page_slot_table % owner_slots
    owner_pool = owner_index % pool_count
    owner_head = owner_index // pool_count % head_count
    owner_ctx = owner_index // (pool_count * head_count)
    location = (
        (owner_ctx * pool_count + owner_pool) * held_slots + owner_head * owner_slots + within
    )
    ordered_keys = jnp.take(plane_keys, location, axis=0).reshape(
        prompts, page_count * page_len, head_dim
    )
    ordered_values = jnp.take(plane_values, location, axis=0).reshape(
        prompts, page_count * page_len, head_dim
    )
    key_span = min(2048, page_count * page_len)
    states = []
    for prompt in range(prompts):
        prefix_len = prefix_lengths[prompt]
        query_page = (prefix_len + row_ids) // page_len
        query_block = queries[prompt].reshape(local_rows, group_size, head_dim)
        prompt_keys = ordered_keys[prompt]
        prompt_values = ordered_values[prompt]

        def prefix_step(block_index, running):
            first_key = block_index * key_span
            key_part = lax.dynamic_slice_in_dim(prompt_keys, first_key, key_span, 0)
            value_part = lax.dynamic_slice_in_dim(prompt_values, first_key, key_span, 0)
            key_ids = first_key + jnp.arange(key_span, dtype=jnp.int32)
            first_page = first_key // page_len
            page_part = lax.dynamic_slice_in_dim(vert_hit, first_page, key_span // page_len, 1)
            distance = (
                query_page[:, None]
                - (first_page + jnp.arange(key_span // page_len, dtype=jnp.int32))[None, :]
            )
            slash_hit = jnp.any(slash_rows[:, :, None, None] == distance[None, None], axis=1)
            chosen = page_part[:, None, :] | slash_hit
            allowed = jnp.repeat(chosen, page_len, axis=2) & (key_ids < prefix_len)[None, None, :]
            scores = (
                jnp.einsum("rgd,kd->grk", query_block, key_part, preferred_element_type=jnp.float32)
                * scaling
            )
            return absorb(running, scores, allowed, value_part)

        upper_bound = (prefix_len + key_span - 1) // key_span
        states.append(lax.fori_loop(0, upper_bound, prefix_step, empty_state))
    plane_stretch_keys, plane_stretch_values = (
        lax.all_gather(stretch_keys, ("ctx", "pool"), axis=1, tiled=True),
        lax.all_gather(stretch_values, ("ctx", "pool"), axis=1, tiled=True),
    )
    stretch_span = min(2048, stretch_len)
    outputs = []
    for prompt in range(prompts):
        query_block = queries[prompt].reshape(local_rows, group_size, head_dim)
        prompt_keys = plane_stretch_keys[prompt]
        prompt_values = plane_stretch_values[prompt]

        def stretch_step(block_index, running):
            first_key = block_index * stretch_span
            key_ids = first_key + jnp.arange(stretch_span, dtype=jnp.int32)
            allowed = jnp.broadcast_to(
                (key_ids[None, :] <= row_ids[:, None])[None], (group_size, local_rows, stretch_span)
            )
            scores = (
                jnp.einsum(
                    "rgd,kd->grk", query_block, prompt_keys, preferred_element_type=jnp.float32
                )
                * scaling
            )
            return absorb(running, scores, allowed, prompt_values)

        upper_bound = (plane_index * local_rows + local_rows - 1) // stretch_span + 1
        highest, totals, numerator = lax.fori_loop(0, upper_bound, stretch_step, states[prompt])
        result = numerator / totals[..., None]
        outputs.append(
            result.transpose(1, 0, 2).reshape(local_rows, row_width).astype(jnp.bfloat16)
        )
    return jnp.stack(outputs)


page_axes = ("ctx", "pool")
hide = -(2.0**126)
scale = 1.4426950408889634 / math.sqrt(128.0)
join_flops = 6 * 10**9
mask_flops = 0
vmem = pl.BlockSpec(memory_space=pltpu.VMEM)
smem = pl.BlockSpec(memory_space=pltpu.SMEM)


def split_kernel(
    pool_keys, pool_values, stretch_keys, stretch_values, first, second, third, early, sems
):
    head = lax.axis_index("head")
    copies = []

    def add(source, target):
        copy = pltpu.make_async_copy(source, target, sems.at[len(copies)])
        copy.start()
        copies.append(copy)

    for shift, target in ((3, third), (2, second), (1, first), (0, None)):
        columns = pl.ds(pl.multiple_of((head ^ shift) * 128, 128), 128)
        for which, pool in enumerate((pool_keys, pool_values)):
            place = early.at[2 + which] if target is None else target.at[which]
            add(pool.at[:, :, columns], place)
    add(stretch_keys, early.at[0])
    add(stretch_values, early.at[1])
    for copy in copies:
        copy.wait()


def split(pool_keys, pool_values, stretch_keys, stretch_values):
    piece = pltpu.VMEM((2, 2, 64, 128), jnp.bfloat16)
    bundle = pltpu.VMEM((4, 2, 64, 128), jnp.bfloat16)
    return pl.pallas_call(
        split_kernel,
        out_shape=(piece, piece, piece, bundle),
        in_specs=[pl.BlockSpec(memory_space=pltpu.HBM)] * 4,
        out_specs=[vmem] * 4,
        scratch_shapes=[pltpu.SemaphoreType.DMA((10,))],
        name="split",
    )(pool_keys, pool_values, stretch_keys, stretch_values)


def join_kernel(first, second, third, joined):
    for index, piece in enumerate((first, second, third)):
        for which in range(2):
            for within in range(2):
                start = index * 128 + within * 64
                joined[which, start : start + 64, :] = piece[which, within]


def join(first, second, third):
    return pl.pallas_call(
        join_kernel,
        out_shape=pltpu.VMEM((2, 384, 128), jnp.bfloat16),
        in_specs=[vmem] * 3,
        out_specs=vmem,
        compiler_params=pltpu.CompilerParams(vmem_limit_bytes=4 * 2**20),
        cost_estimate=pl.CostEstimate(
            flops=join_flops, bytes_accessed=400000, transcendentals=0
        ),
        name="join",
    )(first, second, third)


def mask_kernel(
    lengths_in,
    table_in,
    queries_in,
    vertical_in,
    slash_in,
    wide_queries,
    key_tags,
    meta,
    lengths,
    table,
    queries,
    vertical,
    slash,
    sems,
):
    pairs = (
        (table_in, table),
        (lengths_in, lengths),
        (vertical_in, vertical),
        (slash_in, slash),
        (queries_in, queries),
    )
    copies = []
    for index, (source, target) in enumerate(pairs):
        copies.append(pltpu.make_async_copy(source, target, sems.at[index]))
        copies[-1].start()
    head = lax.axis_index("head")
    plane = lax.axis_index("ctx") * 2 + lax.axis_index("pool")
    first_row = plane * 64
    lane8 = lax.broadcasted_iota(jnp.int32, (8, 128), 1)
    lane = lax.broadcasted_iota(jnp.int32, (64, 128), 1)
    row = lax.broadcasted_iota(jnp.int32, (64, 128), 0)
    causal = jnp.where(lane - 64 <= row, 0.0, hide)
    own_heads = lax.broadcasted_iota(jnp.int32, (8, 32), 0) + head * 8
    pick = (own_heads == lax.broadcasted_iota(jnp.int32, (8, 32), 1)).astype(jnp.float32)
    for page in range(8):
        diagonal = (lane - 64 == row) & (plane == page)
        tag = diagonal | (((lane == 0) | (lane == 32)) & (plane < page))
        start = 4096 + page * 64
        key_tags[start : start + 64, :] = jnp.where(tag, 1.0, 0.0).astype(jnp.bfloat16)
    for copy in copies:
        copy.wait()
    for index in range(64):
        meta[table[index]] = index * 64
    for prompt in range(2):
        meta[64 + prompt] = lengths[prompt]

    def own(entries):
        picked = lax.dot_general(
            pick,
            entries[...].astype(jnp.float32),
            (((1,), (1,)), ((), ())),
            preferred_element_type=jnp.float32,
        )
        return (picked + 0.5).astype(jnp.int32)

    vert_rows, slash_rows = own(vertical), own(slash)
    page8 = lane8 % 32
    vert_hit = lane8 < 0
    for entry in range(16):
        vert_hit = vert_hit | (vert_rows[:, entry : entry + 1] == page8)
    for prompt in range(2):
        length = lengths[prompt]
        base_page = (length + first_row) // 64
        cut = (base_page + 1) * 64 - length - first_row
        tables = []
        for step in range(2):
            hit = vert_hit
            distance = base_page + step - page8
            for entry in range(16):
                hit = hit | (slash_rows[:, entry : entry + 1] == distance)
            shown = hit & (page8 * 64 < length) & (lane8 // 32 == prompt)
            tables.append(jnp.where(shown, 0.0, hide))
        for group in range(8):
            rows = slice(group * 64, (group + 1) * 64)
            bias = jnp.where(
                row < cut, tables[0][group : group + 1, :], tables[1][group : group + 1, :]
            )
            bias = jnp.where(lane < 64, bias, causal)
            wide_queries[prompt, rows, :128] = queries[prompt, :, group * 128 : (group + 1) * 128]
            wide_queries[prompt, rows, 128:] = bias.astype(jnp.bfloat16)
        for page in range(32):
            live = row + page * 64 < length
            tag = (live & (lane == prompt * 32 + page)) | (
                ~live & ((lane == 0) | (lane == 32))
            )
            start = prompt * 2048 + page * 64
            key_tags[start : start + 64, :] = jnp.where(tag, 1.0, 0.0).astype(jnp.bfloat16)


def mask(lengths, table, queries, vertical, slash):
    return pl.pallas_call(
        mask_kernel,
        out_shape=(
            pltpu.VMEM((2, 512, 256), jnp.bfloat16),
            pltpu.VMEM((4608, 128), jnp.bfloat16),
            pltpu.SMEM((72,), jnp.int32),
        ),
        in_specs=[pl.BlockSpec(memory_space=pltpu.HBM)] * 5,
        out_specs=[vmem] * 2 + [smem],
        scratch_shapes=[
            pltpu.SMEM((2,), jnp.int32),
            pltpu.SMEM((64,), jnp.int32),
            pltpu.VMEM((2, 64, 1024), jnp.bfloat16),
            pltpu.VMEM((16, 32), jnp.int32),
            pltpu.VMEM((16, 32), jnp.int32),
            pltpu.SemaphoreType.DMA((5,)),
        ],
        cost_estimate=pl.CostEstimate(
            flops=mask_flops, bytes_accessed=1000, transcendentals=0
        ),
        name="mask",
    )(lengths, table, queries, vertical, slash)


def origin(other, role):
    from_pool = lax.axis_index("pool") ^ other
    return lax.axis_index("ctx") ^ (0, 1 + from_pool, 2 - from_pool, 3)[role], from_pool


def tags_at(meta, key_tags, slot):
    return key_tags[pl.ds(pl.multiple_of(meta[slot], 64), 64), :]


def bundle_pages(meta, key_tags, bundle, other, role):
    from_ctx, from_pool = origin(other, role)
    pages = []
    slot = ((from_ctx * 4 + lax.axis_index("head")) * 2 + from_pool) * 2
    for within in range(2):
        tags = tags_at(meta, key_tags, slot + within)
        pages.append((bundle[2, within], tags, bundle[3, within]))
    return pages


def bundle_stretch(key_tags, bundle, other, role, prompt):
    from_ctx, from_pool = origin(other, role)
    start = pl.multiple_of(4096 + (from_ctx * 2 + from_pool) * 64, 64)
    return [(bundle[0, prompt], key_tags[pl.ds(start, 64), :], bundle[1, prompt])]


def joined_pages(meta, key_tags, pieces, other, role):
    from_ctx, from_pool = origin(other, role)
    pages = []
    for shift in range(1, 4):
        slot = ((from_ctx * 4 + (lax.axis_index("head") ^ shift)) * 2 + from_pool) * 2
        for within in range(2):
            place = slice((shift - 1) * 128 + within * 64, (shift - 1) * 128 + within * 64 + 64)
            tags = tags_at(meta, key_tags, slot + within)
            pages.append((pieces[0, place, :], tags, pieces[1, place, :]))
    return pages


def stack(pages):
    keys = jnp.concatenate([page[0] for page in pages], axis=0)
    tags = jnp.concatenate([page[1] for page in pages], axis=0)
    values = jnp.concatenate([page[2] for page in pages], axis=0)
    ones = jnp.ones(values.shape, jnp.bfloat16)
    return jnp.concatenate([keys, tags], axis=1), jnp.concatenate([values, ones], axis=1)


def absorb_pages(wide_queries, shared, own, state, scores):
    shared_keys, shared_values = stack(shared)
    width = shared_keys.shape[0]
    own = [stack(pages) if pages else None for pages in own]
    highs, results = [], []
    for prompt in range(2):
        high = None
        for start, pair in ((0, (shared_keys,)), (width, own[prompt])):
            if pair is None:
                continue
            found = lax.dot_general(
                wide_queries[prompt],
                pair[0],
                (((1,), (1,)), ((), ())),
                preferred_element_type=jnp.float32,
            )
            scores[prompt, :, start : start + found.shape[1]] = found
            for column in range(0, found.shape[1], 128):
                part = found[:, column : column + 128]
                high = part if high is None else jnp.maximum(high, part)
        if state is not None:
            high = jnp.maximum(high, state[0][prompt])
        highs.append(jnp.max(high, axis=1, keepdims=True))
    for prompt in range(2):
        highest = highs[prompt]
        weights = jnp.exp2((scores[prompt] - highest) * scale).astype(jnp.bfloat16)
        sums = jnp.dot(
            weights[:, :width], shared_values, preferred_element_type=jnp.float32
        )
        if own[prompt] is not None:
            sums += jnp.dot(
                weights[:, width:], own[prompt][1], preferred_element_type=jnp.float32
            )
        numerator, totals = sums[:, :128], sums[:, 128:]
        if state is not None:
            factor = jnp.exp2((state[0][prompt] - highest) * scale)
            numerator = numerator + state[1][prompt, :, :128] * factor
            totals = totals + state[1][prompt, :, 128:] * factor
        results.append((highest, numerator, totals))
    return results


def keep(results, high_out, sums_out):
    for prompt, (highest, numerator, totals) in enumerate(results):
        high_out[prompt] = jnp.broadcast_to(highest, (512, 128))
        sums_out[prompt, :, :128] = numerator
        sums_out[prompt, :, 128:] = totals


def open_kernel(meta, wide_queries, key_tags, *rest):
    bundles, pieces = rest[:6], rest[6:8]
    high_out, sums_out, scores = rest[8:]
    shared, own = [], ([], [])
    for other in range(2):
        for role in range(3):
            bundle = bundles[other * 3 + role]
            shared += bundle_pages(meta, key_tags, bundle, other, role)
            for prompt in range(2):
                own[prompt].extend(bundle_stretch(key_tags, bundle, other, role, prompt))
        shared += joined_pages(meta, key_tags, pieces[other], other, 0)
    keep(absorb_pages(wide_queries, shared, own, None, scores), high_out, sums_out)


def middle_kernel(meta, wide_queries, key_tags, before, given, *rest):
    bundles, pieces = rest[:2], rest[2:6]
    high_out, sums_out, scores = rest[6:]
    shared, own = [], ([], [])
    for other in range(2):
        shared += bundle_pages(meta, key_tags, bundles[other], other, 3)
        for prompt in range(2):
            own[prompt].extend(bundle_stretch(key_tags, bundles[other], other, 3, prompt))
        for role in range(2):
            shared += joined_pages(meta, key_tags, pieces[other * 2 + role], other, 1 + role)
    keep(absorb_pages(wide_queries, shared, own, (before, given), scores), high_out, sums_out)


def close_kernel(meta, wide_queries, key_tags, before, given, mine, theirs, result, scores):
    shared = joined_pages(meta, key_tags, mine, 0, 3) + joined_pages(meta, key_tags, theirs, 1, 3)
    results = absorb_pages(wide_queries, shared, ([], []), (before, given), scores)
    for prompt, (_, numerator, totals) in enumerate(results):
        attended = (numerator / totals).astype(jnp.bfloat16)
        for group in range(8):
            rows = slice(group * 64, (group + 1) * 64)
            result[prompt, :, group * 128 : (group + 1) * 128] = attended[rows, :]


def call(kernel, name, out_shape, keys, *operands):
    single = not isinstance(out_shape, tuple)
    return pl.pallas_call(
        kernel,
        out_shape=out_shape,
        in_specs=[smem] + [vmem] * (len(operands) - 1),
        out_specs=vmem if single else (vmem,) * len(out_shape),
        scratch_shapes=[pltpu.VMEM((2, 512, keys), jnp.float32)],
        compiler_params=pltpu.CompilerParams(vmem_limit_bytes=40 * 2**20),
        cost_estimate=pl.CostEstimate(flops=0, bytes_accessed=1000, transcendentals=0),
        name=name,
    )(*operands)


def running():
    return (pltpu.VMEM((2, 512, 128), jnp.float32), pltpu.VMEM((2, 512, 256), jnp.float32))


def open_stage(meta, wide_queries, key_tags, bundles, pieces):
    return call(
        open_kernel, "open", running(), 30 * 64, meta, wide_queries, key_tags, *bundles, *pieces
    )


def middle_stage(meta, wide_queries, key_tags, state, bundles, pieces):
    return call(
        middle_kernel, "middle", running(), 30 * 64,
        meta, wide_queries, key_tags, *state, *bundles, *pieces,
    )


def close_stage(meta, wide_queries, key_tags, state, mine, theirs):
    return call(
        close_kernel, "close", jax.ShapeDtypeStruct((2, 64, 1024), jnp.bfloat16), 12 * 64,
        meta, wide_queries, key_tags, *state, mine, theirs,
    )


def to_first(value):
    pairs = [(2 * c + p, 2 * (c ^ (1 + p)) + p) for c in range(4) for p in range(2)]
    return lax.ppermute(value, page_axes, pairs)


def to_second(value):
    pairs = [(2 * c + p, 2 * (c ^ (2 - p)) + p) for c in range(4) for p in range(2)]
    return lax.ppermute(value, page_axes, pairs)


def to_sibling(value):
    return lax.ppermute(value, "pool", [(0, 1), (1, 0)])


def small_body(
    queries,
    stretch_keys,
    stretch_values,
    slot_pool_keys,
    slot_pool_values,
    prefix_lengths,
    page_slot_table,
    vertical,
    slash,
):
    first, second, third, bundle = split(
        slot_pool_keys, slot_pool_values, stretch_keys, stretch_values
    )
    third, second, first = (
        lax.ppermute(piece, "head", [(z, z ^ shift) for z in range(4)])
        for shift, piece in ((3, third), (2, second), (1, first))
    )
    by_first, by_second = to_first(bundle), to_second(bundle)
    first, lengths = lax.optimization_barrier((first, prefix_lengths))
    masks = mask(lengths, page_slot_table, queries, vertical.T, slash.T)
    first, second, third, masks = lax.optimization_barrier((first, second, third, masks))
    joined = join(first, second, third)
    wide_queries, key_tags, meta = masks
    late_first, late_second = to_first(joined), to_second(joined)
    by_both = to_second(by_first)
    early = [bundle, by_first, by_second]
    early += [to_sibling(one) for one in early]
    state = open_stage(meta, wide_queries, key_tags, early, [joined, to_sibling(joined)])
    late_first, late_second, state = lax.optimization_barrier((late_first, late_second, state))
    late_both = to_second(late_first)
    late = [late_first, late_second]
    late += [to_sibling(one) for one in late]
    state = middle_stage(
        meta, wide_queries, key_tags, state, [by_both, to_sibling(by_both)], late
    )
    state, late_both = lax.optimization_barrier((state, late_both))
    return close_stage(
        meta, wide_queries, key_tags, state, late_both, to_sibling(late_both)
    )


def solution(mesh):
    small = tuple(mesh.shape[axis] for axis in ("ctx", "head", "pool")) == (4, 4, 2)
    in_specs = (
        P(None, ("ctx", "pool"), "head"),
        P(None, ("ctx", "pool"), "head"),
        P(None, ("ctx", "pool"), "head"),
        P(("ctx", "head", "pool"), None, None),
        P(("ctx", "head", "pool"), None, None),
        P(),
        P(),
        P(),
        P(),
    )
    out_specs = P(None, ("ctx", "pool"), "head")
    return jax.shard_map(
        small_body if small else body,
        mesh=mesh,
        in_specs=in_specs,
        out_specs=out_specs,
        check_vma=False,
    )
```

```python
import math

import jax
import jax.numpy as jnp
from jax import lax
from jax.experimental import pallas as pl
from jax.experimental.pallas import tpu as pltpu
from jax.sharding import PartitionSpec as P

very_low = -1e30


def absorb(running, scores, allowed, values):
    highest, totals, numerator = running
    new_high = jnp.maximum(highest, jnp.max(jnp.where(allowed, scores, very_low), axis=-1))
    factor = jnp.exp(highest - new_high)
    weights = jnp.where(allowed, jnp.exp(scores - new_high[..., None]), 0.0)
    totals = totals * factor + jnp.sum(weights, axis=-1)
    numerator = numerator * factor[..., None] + jnp.einsum(
        "grk,kd->grd", weights.astype(jnp.bfloat16), values, preferred_element_type=jnp.float32
    )
    return (new_high, totals, numerator)


def body(
    queries,
    stretch_keys,
    stretch_values,
    slot_pool_keys,
    slot_pool_values,
    prefix_lengths,
    page_slot_table,
    vertical,
    slash,
):
    prompts, local_rows, row_width = queries.shape
    head_dim = stretch_keys.shape[2]
    group_size = row_width // head_dim
    page_len = slot_pool_keys.shape[1]
    owner_slots = slot_pool_keys.shape[0]
    slot_total = page_slot_table.shape[0]
    page_count = slot_total // prompts
    head_count = lax.axis_size("head")
    pool_count = lax.axis_size("pool")
    ctx_count = lax.axis_size("ctx")
    plane_size = ctx_count * pool_count
    ctx_index = lax.axis_index("ctx")
    pool_index = lax.axis_index("pool")
    head_index = lax.axis_index("head")
    plane_index = ctx_index * pool_count + pool_index
    stretch_len = plane_size * local_rows
    scaling = 1.0 / math.sqrt(head_dim)
    vert_rows = lax.dynamic_slice_in_dim(vertical, head_index * group_size, group_size, 0)
    slash_rows = lax.dynamic_slice_in_dim(slash, head_index * group_size, group_size, 0)
    page_ids = jnp.arange(page_count, dtype=jnp.int32)
    vert_hit = jnp.any(vert_rows[:, :, None] == page_ids[None, None, :], axis=1)
    row_ids = plane_index * local_rows + jnp.arange(local_rows, dtype=jnp.int32)
    page_keys, page_values = (
        lax.all_to_all(slot_pool_keys, "head", split_axis=2, concat_axis=0, tiled=True),
        lax.all_to_all(slot_pool_values, "head", split_axis=2, concat_axis=0, tiled=True),
    )
    held_slots = owner_slots * head_count
    empty_state = (
        jnp.full((group_size, local_rows), very_low, jnp.float32),
        jnp.zeros((group_size, local_rows), jnp.float32),
        jnp.zeros((group_size, local_rows, head_dim), jnp.float32),
    )
    plane_keys, plane_values = (
        lax.all_gather(page_keys, ("ctx", "pool"), axis=0, tiled=True),
        lax.all_gather(page_values, ("ctx", "pool"), axis=0, tiled=True),
    )
    owner_index = page_slot_table // owner_slots
    within = page_slot_table % owner_slots
    owner_pool = owner_index % pool_count
    owner_head = owner_index // pool_count % head_count
    owner_ctx = owner_index // (pool_count * head_count)
    location = (
        (owner_ctx * pool_count + owner_pool) * held_slots + owner_head * owner_slots + within
    )
    ordered_keys = jnp.take(plane_keys, location, axis=0).reshape(
        prompts, page_count * page_len, head_dim
    )
    ordered_values = jnp.take(plane_values, location, axis=0).reshape(
        prompts, page_count * page_len, head_dim
    )
    key_span = min(2048, page_count * page_len)
    states = []
    for prompt in range(prompts):
        prefix_len = prefix_lengths[prompt]
        query_page = (prefix_len + row_ids) // page_len
        query_block = queries[prompt].reshape(local_rows, group_size, head_dim)
        prompt_keys = ordered_keys[prompt]
        prompt_values = ordered_values[prompt]

        def prefix_step(block_index, running):
            first_key = block_index * key_span
            key_part = lax.dynamic_slice_in_dim(prompt_keys, first_key, key_span, 0)
            value_part = lax.dynamic_slice_in_dim(prompt_values, first_key, key_span, 0)
            key_ids = first_key + jnp.arange(key_span, dtype=jnp.int32)
            first_page = first_key // page_len
            page_part = lax.dynamic_slice_in_dim(vert_hit, first_page, key_span // page_len, 1)
            distance = (
                query_page[:, None]
                - (first_page + jnp.arange(key_span // page_len, dtype=jnp.int32))[None, :]
            )
            slash_hit = jnp.any(slash_rows[:, :, None, None] == distance[None, None], axis=1)
            chosen = page_part[:, None, :] | slash_hit
            allowed = jnp.repeat(chosen, page_len, axis=2) & (key_ids < prefix_len)[None, None, :]
            scores = (
                jnp.einsum("rgd,kd->grk", query_block, key_part, preferred_element_type=jnp.float32)
                * scaling
            )
            return absorb(running, scores, allowed, value_part)

        upper_bound = (prefix_len + key_span - 1) // key_span
        states.append(lax.fori_loop(0, upper_bound, prefix_step, empty_state))
    plane_stretch_keys, plane_stretch_values = (
        lax.all_gather(stretch_keys, ("ctx", "pool"), axis=1, tiled=True),
        lax.all_gather(stretch_values, ("ctx", "pool"), axis=1, tiled=True),
    )
    stretch_span = min(2048, stretch_len)
    outputs = []
    for prompt in range(prompts):
        query_block = queries[prompt].reshape(local_rows, group_size, head_dim)
        prompt_keys = plane_stretch_keys[prompt]
        prompt_values = plane_stretch_values[prompt]

        def stretch_step(block_index, running):
            first_key = block_index * stretch_span
            key_ids = first_key + jnp.arange(stretch_span, dtype=jnp.int32)
            allowed = jnp.broadcast_to(
                (key_ids[None, :] <= row_ids[:, None])[None], (group_size, local_rows, stretch_span)
            )
            scores = (
                jnp.einsum(
                    "rgd,kd->grk", query_block, prompt_keys, preferred_element_type=jnp.float32
                )
                * scaling
            )
            return absorb(running, scores, allowed, prompt_values)

        upper_bound = (plane_index * local_rows + local_rows - 1) // stretch_span + 1
        highest, totals, numerator = lax.fori_loop(0, upper_bound, stretch_step, states[prompt])
        result = numerator / totals[..., None]
        outputs.append(
            result.transpose(1, 0, 2).reshape(local_rows, row_width).astype(jnp.bfloat16)
        )
    return jnp.stack(outputs)


page_axes = ("ctx", "pool")
hide = -(2.0**126)
scale = 1.4426950408889634 / math.sqrt(128.0)
join_flops = 6 * 10**9
mask_flops = 0
vmem = pl.BlockSpec(memory_space=pltpu.VMEM)
smem = pl.BlockSpec(memory_space=pltpu.SMEM)


def split_kernel(
    pool_keys, pool_values, stretch_keys, stretch_values, third, second, first, early, sems
):
    head = lax.axis_index("head")
    copies = []

    def add(source, target):
        copy = pltpu.make_async_copy(source, target, sems.at[len(copies)])
        copy.start()
        copies.append(copy)

    for shift, target in ((3, third), (2, second), (1, first), (0, None)):
        columns = pl.ds(pl.multiple_of((head ^ shift) * 128, 128), 128)
        for which, pool in enumerate((pool_keys, pool_values)):
            place = early.at[2 + which] if target is None else target.at[which]
            add(pool.at[:, :, columns], place)
    add(stretch_keys, early.at[0])
    add(stretch_values, early.at[1])
    for copy in copies:
        copy.wait()


def split(pool_keys, pool_values, stretch_keys, stretch_values):
    piece = pltpu.VMEM((2, 2, 64, 128), jnp.bfloat16)
    bundle = pltpu.VMEM((4, 2, 64, 128), jnp.bfloat16)
    return pl.pallas_call(
        split_kernel,
        out_shape=(piece, piece, piece, bundle),
        in_specs=[pl.BlockSpec(memory_space=pltpu.HBM)] * 4,
        out_specs=[vmem] * 4,
        scratch_shapes=[pltpu.SemaphoreType.DMA((10,))],
        name="split",
    )(pool_keys, pool_values, stretch_keys, stretch_values)


def join_kernel(third, second, first, joined):
    for index, piece in enumerate((first, second, third)):
        for which in range(2):
            for within in range(2):
                start = index * 128 + within * 64
                joined[which, start : start + 64, :] = piece[which, within]


def join(third, second, first):
    return pl.pallas_call(
        join_kernel,
        out_shape=pltpu.VMEM((2, 384, 128), jnp.bfloat16),
        in_specs=[vmem] * 3,
        out_specs=vmem,
        compiler_params=pltpu.CompilerParams(vmem_limit_bytes=4 * 2**20),
        cost_estimate=pl.CostEstimate(
            flops=join_flops, bytes_accessed=400000, transcendentals=0
        ),
        name="join",
    )(third, second, first)


def mask_kernel(
    lengths_in,
    table_in,
    queries_in,
    vertical_in,
    slash_in,
    wide_queries,
    key_tags,
    meta,
    lengths,
    table,
    queries,
    vertical,
    slash,
    sems,
):
    pairs = (
        (table_in, table),
        (lengths_in, lengths),
        (vertical_in, vertical),
        (slash_in, slash),
        (queries_in, queries),
    )
    copies = []
    for index, (source, target) in enumerate(pairs):
        copies.append(pltpu.make_async_copy(source, target, sems.at[index]))
        copies[-1].start()
    head = lax.axis_index("head")
    plane = lax.axis_index("ctx") * 2 + lax.axis_index("pool")
    first_row = plane * 64
    lane8 = lax.broadcasted_iota(jnp.int32, (8, 128), 1)
    lane = lax.broadcasted_iota(jnp.int32, (64, 128), 1)
    row = lax.broadcasted_iota(jnp.int32, (64, 128), 0)
    causal = jnp.where(lane - 64 <= row, 0.0, hide)
    hidden = jnp.where((lane == 0) | (lane == 32), 1.0, 0.0)
    own_heads = lax.broadcasted_iota(jnp.int32, (8, 32), 0) + head * 8
    pick = (own_heads == lax.broadcasted_iota(jnp.int32, (8, 32), 1)).astype(jnp.float32)
    for page in range(8):
        diagonal = (lane - 64 == row) & (plane == page)
        tag = diagonal | (((lane == 0) | (lane == 32)) & (plane < page))
        start = 4096 + page * 64
        key_tags[start : start + 64, :] = jnp.where(tag, 1.0, 0.0).astype(jnp.bfloat16)
    for copy in copies:
        copy.wait()
    for index in range(64):
        meta[table[index]] = index * 64
    for prompt in range(2):
        meta[64 + prompt] = lengths[prompt]

    def own(entries):
        picked = lax.dot_general(
            pick,
            entries[...].astype(jnp.float32),
            (((1,), (1,)), ((), ())),
            preferred_element_type=jnp.float32,
        )
        return (picked + 0.5).astype(jnp.int32)

    vert_rows, slash_rows = own(vertical), own(slash)
    page8 = lane8 % 32
    vert_hit = lane8 < 0
    for entry in range(16):
        vert_hit = vert_hit | (vert_rows[:, entry : entry + 1] == page8)
    for prompt in range(2):
        length = lengths[prompt]
        base_page = (length + first_row) // 64
        cut = (base_page + 1) * 64 - length - first_row
        tables = []
        for step in range(2):
            hit = vert_hit
            distance = base_page + step - page8
            for entry in range(16):
                hit = hit | (slash_rows[:, entry : entry + 1] == distance)
            shown = hit & (page8 * 64 < length) & (lane8 // 32 == prompt)
            tables.append(jnp.where(shown, 0.0, hide))
        for group in range(8):
            rows = slice(group * 64, (group + 1) * 64)
            bias = jnp.where(
                row < cut, tables[0][group : group + 1, :], tables[1][group : group + 1, :]
            )
            bias = jnp.where(lane < 64, bias, causal)
            wide_queries[prompt, rows, :128] = queries[prompt, :, group * 128 : (group + 1) * 128]
            wide_queries[prompt, rows, 128:] = bias.astype(jnp.bfloat16)
        for page in range(32):
            tag = jnp.where(lane[:16] == prompt * 32 + page, 1.0, 0.0)
            tag = jnp.where(page * 64 < length, tag, hidden[:16]).astype(jnp.bfloat16)
            start = prompt * 2048 + page * 64
            key_tags[start : start + 64, :] = jnp.concatenate([tag] * 4, axis=0)
        page = jnp.minimum(length // 64, 31)
        tag = jnp.where(lane == prompt * 32 + page, 1.0, 0.0)
        tag = jnp.where(row + page * 64 < length, tag, hidden).astype(jnp.bfloat16)
        key_tags[pl.ds(pl.multiple_of(prompt * 2048 + page * 64, 64), 64), :] = tag


def mask(lengths, table, queries, vertical, slash):
    return pl.pallas_call(
        mask_kernel,
        out_shape=(
            pltpu.VMEM((2, 512, 256), jnp.bfloat16),
            pltpu.VMEM((4608, 128), jnp.bfloat16),
            pltpu.SMEM((72,), jnp.int32),
        ),
        in_specs=[pl.BlockSpec(memory_space=pltpu.HBM)] * 5,
        out_specs=[vmem] * 2 + [smem],
        scratch_shapes=[
            pltpu.SMEM((2,), jnp.int32),
            pltpu.SMEM((64,), jnp.int32),
            pltpu.VMEM((2, 64, 1024), jnp.bfloat16),
            pltpu.VMEM((16, 32), jnp.int32),
            pltpu.VMEM((16, 32), jnp.int32),
            pltpu.SemaphoreType.DMA((5,)),
        ],
        cost_estimate=pl.CostEstimate(
            flops=mask_flops, bytes_accessed=1000, transcendentals=0
        ),
        name="mask",
    )(lengths, table, queries, vertical, slash)


def origin(other, role):
    from_pool = lax.axis_index("pool") ^ other
    return lax.axis_index("ctx") ^ (0, 1 + from_pool, 2 - from_pool, 3)[role], from_pool


def tags_at(meta, key_tags, slot):
    return key_tags[pl.ds(pl.multiple_of(meta[slot], 64), 64), :]


def bundle_pages(meta, key_tags, bundle, other, role):
    from_ctx, from_pool = origin(other, role)
    pages = []
    slot = ((from_ctx * 4 + lax.axis_index("head")) * 2 + from_pool) * 2
    for within in range(2):
        tags = tags_at(meta, key_tags, slot + within)
        pages.append((bundle[2, within], tags, bundle[3, within]))
    return pages


def bundle_stretch(key_tags, bundle, other, role, prompt):
    from_ctx, from_pool = origin(other, role)
    start = pl.multiple_of(4096 + (from_ctx * 2 + from_pool) * 64, 64)
    return [(bundle[0, prompt], key_tags[pl.ds(start, 64), :], bundle[1, prompt])]


def joined_pages(meta, key_tags, pieces, other, role):
    from_ctx, from_pool = origin(other, role)
    pages = []
    for shift in range(1, 4):
        slot = ((from_ctx * 4 + (lax.axis_index("head") ^ shift)) * 2 + from_pool) * 2
        for within in range(2):
            place = slice((shift - 1) * 128 + within * 64, (shift - 1) * 128 + within * 64 + 64)
            tags = tags_at(meta, key_tags, slot + within)
            pages.append((pieces[0, place, :], tags, pieces[1, place, :]))
    return pages


def stack(pages):
    keys = jnp.concatenate([page[0] for page in pages], axis=0)
    tags = jnp.concatenate([page[1] for page in pages], axis=0)
    values = jnp.concatenate([page[2] for page in pages], axis=0)
    ones = jnp.ones(values.shape, jnp.bfloat16)
    return jnp.concatenate([keys, tags], axis=1), jnp.concatenate([values, ones], axis=1)


def absorb_pages(wide_queries, shared, own, state, scores):
    shared_keys, shared_values = stack(shared)
    width = shared_keys.shape[0]
    own = [stack(pages) if pages else None for pages in own]
    highs, results = [], []
    for prompt in range(2):
        high = None
        for start, pair in ((0, (shared_keys,)), (width, own[prompt])):
            if pair is None:
                continue
            found = lax.dot_general(
                wide_queries[prompt],
                pair[0],
                (((1,), (1,)), ((), ())),
                preferred_element_type=jnp.float32,
            )
            scores[prompt, :, start : start + found.shape[1]] = found
            for column in range(0, found.shape[1], 128):
                part = found[:, column : column + 128]
                high = part if high is None else jnp.maximum(high, part)
        if state is not None:
            high = jnp.maximum(high, state[0][prompt])
        highs.append(jnp.max(high, axis=1, keepdims=True))
    for prompt in range(2):
        highest = highs[prompt]
        weights = jnp.exp2((scores[prompt] - highest) * scale).astype(jnp.bfloat16)
        sums = jnp.dot(
            weights[:, :width], shared_values, preferred_element_type=jnp.float32
        )
        if own[prompt] is not None:
            sums += jnp.dot(
                weights[:, width:], own[prompt][1], preferred_element_type=jnp.float32
            )
        numerator, totals = sums[:, :128], sums[:, 128:]
        if state is not None:
            factor = jnp.exp2((state[0][prompt] - highest) * scale)
            numerator = numerator + state[1][prompt, :, :128] * factor
            totals = totals + state[1][prompt, :, 128:] * factor
        results.append((highest, numerator, totals))
    return results


def keep(results, high_out, sums_out):
    for prompt, (highest, numerator, totals) in enumerate(results):
        high_out[prompt] = jnp.broadcast_to(highest, (512, 128))
        sums_out[prompt, :, :128] = numerator
        sums_out[prompt, :, 128:] = totals


def open_kernel(meta, wide_queries, key_tags, *rest):
    bundles, pieces = rest[:6], rest[6:8]
    high_out, sums_out, scores = rest[8:]
    shared, own = [], ([], [])
    for other in range(2):
        for role in range(3):
            bundle = bundles[other * 3 + role]
            shared += bundle_pages(meta, key_tags, bundle, other, role)
            for prompt in range(2):
                own[prompt].extend(bundle_stretch(key_tags, bundle, other, role, prompt))
        shared += joined_pages(meta, key_tags, pieces[other], other, 0)
    keep(absorb_pages(wide_queries, shared, own, None, scores), high_out, sums_out)


def middle_kernel(meta, wide_queries, key_tags, before, given, *rest):
    bundles, pieces = rest[:2], rest[2:6]
    high_out, sums_out, scores = rest[6:]
    shared, own = [], ([], [])
    for other in range(2):
        shared += bundle_pages(meta, key_tags, bundles[other], other, 3)
        for prompt in range(2):
            own[prompt].extend(bundle_stretch(key_tags, bundles[other], other, 3, prompt))
        for role in range(2):
            shared += joined_pages(meta, key_tags, pieces[other * 2 + role], other, 1 + role)
    keep(absorb_pages(wide_queries, shared, own, (before, given), scores), high_out, sums_out)


def close_kernel(meta, wide_queries, key_tags, before, given, mine, theirs, result, scores):
    shared = joined_pages(meta, key_tags, mine, 0, 3) + joined_pages(meta, key_tags, theirs, 1, 3)
    results = absorb_pages(wide_queries, shared, ([], []), (before, given), scores)
    for prompt, (_, numerator, totals) in enumerate(results):
        attended = (numerator / totals).astype(jnp.bfloat16)
        for group in range(8):
            rows = slice(group * 64, (group + 1) * 64)
            result[prompt, :, group * 128 : (group + 1) * 128] = attended[rows, :]


def call(kernel, name, out_shape, keys, *operands):
    single = not isinstance(out_shape, tuple)
    return pl.pallas_call(
        kernel,
        out_shape=out_shape,
        in_specs=[smem] + [vmem] * (len(operands) - 1),
        out_specs=vmem if single else (vmem,) * len(out_shape),
        scratch_shapes=[pltpu.VMEM((2, 512, keys), jnp.float32)],
        compiler_params=pltpu.CompilerParams(vmem_limit_bytes=40 * 2**20),
        cost_estimate=pl.CostEstimate(flops=0, bytes_accessed=1000, transcendentals=0),
        name=name,
    )(*operands)


def running():
    return (pltpu.VMEM((2, 512, 128), jnp.float32), pltpu.VMEM((2, 512, 256), jnp.float32))


def open_stage(meta, wide_queries, key_tags, bundles, pieces):
    return call(
        open_kernel, "open", running(), 30 * 64, meta, wide_queries, key_tags, *bundles, *pieces
    )


def middle_stage(meta, wide_queries, key_tags, state, bundles, pieces):
    return call(
        middle_kernel, "middle", running(), 30 * 64,
        meta, wide_queries, key_tags, *state, *bundles, *pieces,
    )


def close_stage(meta, wide_queries, key_tags, state, mine, theirs):
    return call(
        close_kernel, "close", jax.ShapeDtypeStruct((2, 64, 1024), jnp.bfloat16), 12 * 64,
        meta, wide_queries, key_tags, *state, mine, theirs,
    )


def to_first(value):
    pairs = [(2 * c + p, 2 * (c ^ (1 + p)) + p) for c in range(4) for p in range(2)]
    return lax.ppermute(value, page_axes, pairs)


def to_second(value):
    pairs = [(2 * c + p, 2 * (c ^ (2 - p)) + p) for c in range(4) for p in range(2)]
    return lax.ppermute(value, page_axes, pairs)


def to_sibling(value):
    return lax.ppermute(value, "pool", [(0, 1), (1, 0)])


def small_body(
    queries,
    stretch_keys,
    stretch_values,
    slot_pool_keys,
    slot_pool_values,
    prefix_lengths,
    page_slot_table,
    vertical,
    slash,
):
    third, second, first, bundle = split(
        slot_pool_keys, slot_pool_values, stretch_keys, stretch_values
    )
    third, second, first = (
        lax.ppermute(piece, "head", [(z, z ^ shift) for z in range(4)])
        for shift, piece in ((3, third), (2, second), (1, first))
    )
    by_first, by_second = to_first(bundle), to_second(bundle)
    third, lengths = lax.optimization_barrier((third, prefix_lengths))
    masks = mask(lengths, page_slot_table, queries, vertical.T, slash.T)
    third, second, first, masks = lax.optimization_barrier((third, second, first, masks))
    joined = join(third, second, first)
    wide_queries, key_tags, meta = masks
    late_first, late_second = to_first(joined), to_second(joined)
    by_both = to_second(by_first)
    early = [bundle, by_first, by_second]
    early += [to_sibling(one) for one in early]
    state = open_stage(meta, wide_queries, key_tags, early, [joined, to_sibling(joined)])
    late_first, late_second, state = lax.optimization_barrier((late_first, late_second, state))
    late_both = to_second(late_first)
    late = [late_first, late_second]
    late += [to_sibling(one) for one in late]
    state = middle_stage(
        meta, wide_queries, key_tags, state, [by_both, to_sibling(by_both)], late
    )
    state, late_both = lax.optimization_barrier((state, late_both))
    return close_stage(
        meta, wide_queries, key_tags, state, late_both, to_sibling(late_both)
    )


def solution(mesh):
    small = tuple(mesh.shape[axis] for axis in ("ctx", "head", "pool")) == (4, 4, 2)
    in_specs = (
        P(None, ("ctx", "pool"), "head"),
        P(None, ("ctx", "pool"), "head"),
        P(None, ("ctx", "pool"), "head"),
        P(("ctx", "head", "pool"), None, None),
        P(("ctx", "head", "pool"), None, None),
        P(),
        P(),
        P(),
        P(),
    )
    out_specs = P(None, ("ctx", "pool"), "head")
    return jax.shard_map(
        small_body if small else body,
        mesh=mesh,
        in_specs=in_specs,
        out_specs=out_specs,
        check_vma=False,
    )
```

```python
import math

import jax
import jax.numpy as jnp
from jax import lax
from jax.experimental import pallas as pl
from jax.experimental.pallas import tpu as pltpu
from jax.sharding import PartitionSpec as P

very_low = -1e30


def absorb(running, scores, allowed, values):
    highest, totals, numerator = running
    new_high = jnp.maximum(highest, jnp.max(jnp.where(allowed, scores, very_low), axis=-1))
    factor = jnp.exp(highest - new_high)
    weights = jnp.where(allowed, jnp.exp(scores - new_high[..., None]), 0.0)
    totals = totals * factor + jnp.sum(weights, axis=-1)
    numerator = numerator * factor[..., None] + jnp.einsum(
        "grk,kd->grd", weights.astype(jnp.bfloat16), values, preferred_element_type=jnp.float32
    )
    return (new_high, totals, numerator)


def body(
    queries,
    stretch_keys,
    stretch_values,
    slot_pool_keys,
    slot_pool_values,
    prefix_lengths,
    page_slot_table,
    vertical,
    slash,
):
    prompts, local_rows, row_width = queries.shape
    head_dim = stretch_keys.shape[2]
    group_size = row_width // head_dim
    page_len = slot_pool_keys.shape[1]
    owner_slots = slot_pool_keys.shape[0]
    slot_total = page_slot_table.shape[0]
    page_count = slot_total // prompts
    head_count = lax.axis_size("head")
    pool_count = lax.axis_size("pool")
    ctx_count = lax.axis_size("ctx")
    plane_size = ctx_count * pool_count
    ctx_index = lax.axis_index("ctx")
    pool_index = lax.axis_index("pool")
    head_index = lax.axis_index("head")
    plane_index = ctx_index * pool_count + pool_index
    stretch_len = plane_size * local_rows
    scaling = 1.0 / math.sqrt(head_dim)
    vert_rows = lax.dynamic_slice_in_dim(vertical, head_index * group_size, group_size, 0)
    slash_rows = lax.dynamic_slice_in_dim(slash, head_index * group_size, group_size, 0)
    page_ids = jnp.arange(page_count, dtype=jnp.int32)
    vert_hit = jnp.any(vert_rows[:, :, None] == page_ids[None, None, :], axis=1)
    row_ids = plane_index * local_rows + jnp.arange(local_rows, dtype=jnp.int32)
    page_keys, page_values = (
        lax.all_to_all(slot_pool_keys, "head", split_axis=2, concat_axis=0, tiled=True),
        lax.all_to_all(slot_pool_values, "head", split_axis=2, concat_axis=0, tiled=True),
    )
    held_slots = owner_slots * head_count
    empty_state = (
        jnp.full((group_size, local_rows), very_low, jnp.float32),
        jnp.zeros((group_size, local_rows), jnp.float32),
        jnp.zeros((group_size, local_rows, head_dim), jnp.float32),
    )
    plane_keys, plane_values = (
        lax.all_gather(page_keys, ("ctx", "pool"), axis=0, tiled=True),
        lax.all_gather(page_values, ("ctx", "pool"), axis=0, tiled=True),
    )
    owner_index = page_slot_table // owner_slots
    within = page_slot_table % owner_slots
    owner_pool = owner_index % pool_count
    owner_head = owner_index // pool_count % head_count
    owner_ctx = owner_index // (pool_count * head_count)
    location = (
        (owner_ctx * pool_count + owner_pool) * held_slots + owner_head * owner_slots + within
    )
    ordered_keys = jnp.take(plane_keys, location, axis=0).reshape(
        prompts, page_count * page_len, head_dim
    )
    ordered_values = jnp.take(plane_values, location, axis=0).reshape(
        prompts, page_count * page_len, head_dim
    )
    key_span = min(2048, page_count * page_len)
    states = []
    for prompt in range(prompts):
        prefix_len = prefix_lengths[prompt]
        query_page = (prefix_len + row_ids) // page_len
        query_block = queries[prompt].reshape(local_rows, group_size, head_dim)
        prompt_keys = ordered_keys[prompt]
        prompt_values = ordered_values[prompt]

        def prefix_step(block_index, running):
            first_key = block_index * key_span
            key_part = lax.dynamic_slice_in_dim(prompt_keys, first_key, key_span, 0)
            value_part = lax.dynamic_slice_in_dim(prompt_values, first_key, key_span, 0)
            key_ids = first_key + jnp.arange(key_span, dtype=jnp.int32)
            first_page = first_key // page_len
            page_part = lax.dynamic_slice_in_dim(vert_hit, first_page, key_span // page_len, 1)
            distance = (
                query_page[:, None]
                - (first_page + jnp.arange(key_span // page_len, dtype=jnp.int32))[None, :]
            )
            slash_hit = jnp.any(slash_rows[:, :, None, None] == distance[None, None], axis=1)
            chosen = page_part[:, None, :] | slash_hit
            allowed = jnp.repeat(chosen, page_len, axis=2) & (key_ids < prefix_len)[None, None, :]
            scores = (
                jnp.einsum("rgd,kd->grk", query_block, key_part, preferred_element_type=jnp.float32)
                * scaling
            )
            return absorb(running, scores, allowed, value_part)

        upper_bound = (prefix_len + key_span - 1) // key_span
        states.append(lax.fori_loop(0, upper_bound, prefix_step, empty_state))
    plane_stretch_keys, plane_stretch_values = (
        lax.all_gather(stretch_keys, ("ctx", "pool"), axis=1, tiled=True),
        lax.all_gather(stretch_values, ("ctx", "pool"), axis=1, tiled=True),
    )
    stretch_span = min(2048, stretch_len)
    outputs = []
    for prompt in range(prompts):
        query_block = queries[prompt].reshape(local_rows, group_size, head_dim)
        prompt_keys = plane_stretch_keys[prompt]
        prompt_values = plane_stretch_values[prompt]

        def stretch_step(block_index, running):
            first_key = block_index * stretch_span
            key_ids = first_key + jnp.arange(stretch_span, dtype=jnp.int32)
            allowed = jnp.broadcast_to(
                (key_ids[None, :] <= row_ids[:, None])[None], (group_size, local_rows, stretch_span)
            )
            scores = (
                jnp.einsum(
                    "rgd,kd->grk", query_block, prompt_keys, preferred_element_type=jnp.float32
                )
                * scaling
            )
            return absorb(running, scores, allowed, prompt_values)

        upper_bound = (plane_index * local_rows + local_rows - 1) // stretch_span + 1
        highest, totals, numerator = lax.fori_loop(0, upper_bound, stretch_step, states[prompt])
        result = numerator / totals[..., None]
        outputs.append(
            result.transpose(1, 0, 2).reshape(local_rows, row_width).astype(jnp.bfloat16)
        )
    return jnp.stack(outputs)


page_axes = ("ctx", "pool")
hide = -(2.0**126)
scale = 1.4426950408889634 / math.sqrt(128.0)
join_flops = 6 * 10**9
mask_flops = 0
beside_flops = 20 * 10**8
vmem = pl.BlockSpec(memory_space=pltpu.VMEM)
smem = pl.BlockSpec(memory_space=pltpu.SMEM)


def split_kernel(
    pool_keys, pool_values, stretch_keys, stretch_values, third, second, first, early, sems
):
    head = lax.axis_index("head")
    copies = []

    def add(source, target):
        copy = pltpu.make_async_copy(source, target, sems.at[len(copies)])
        copy.start()
        copies.append(copy)

    for shift, target in ((3, third), (2, second), (1, first), (0, None)):
        columns = pl.ds(pl.multiple_of((head ^ shift) * 128, 128), 128)
        for which, pool in enumerate((pool_keys, pool_values)):
            place = early.at[2 + which] if target is None else target.at[which]
            add(pool.at[:, :, columns], place)
    add(stretch_keys, early.at[0])
    add(stretch_values, early.at[1])
    for copy in copies:
        copy.wait()


def split(pool_keys, pool_values, stretch_keys, stretch_values):
    piece = pltpu.VMEM((2, 2, 64, 128), jnp.bfloat16)
    bundle = pltpu.VMEM((4, 2, 64, 128), jnp.bfloat16)
    return pl.pallas_call(
        split_kernel,
        out_shape=(piece, piece, piece, bundle),
        in_specs=[pl.BlockSpec(memory_space=pltpu.HBM)] * 4,
        out_specs=[vmem] * 4,
        scratch_shapes=[pltpu.SemaphoreType.DMA((10,))],
        name="split",
    )(pool_keys, pool_values, stretch_keys, stretch_values)


def join_kernel(third, second, first, joined):
    for index, piece in enumerate((first, second, third)):
        for which in range(2):
            for within in range(2):
                start = index * 128 + within * 64
                joined[which, start : start + 64, :] = piece[which, within]


def join(third, second, first):
    return pl.pallas_call(
        join_kernel,
        out_shape=pltpu.VMEM((2, 384, 128), jnp.bfloat16),
        in_specs=[vmem] * 3,
        out_specs=vmem,
        compiler_params=pltpu.CompilerParams(vmem_limit_bytes=4 * 2**20),
        cost_estimate=pl.CostEstimate(
            flops=join_flops, bytes_accessed=400000, transcendentals=0
        ),
        name="join",
    )(third, second, first)


def mask_kernel(
    lengths_in,
    table_in,
    queries_in,
    vertical_in,
    slash_in,
    wide_queries,
    key_tags,
    meta,
    lengths,
    table,
    queries,
    vertical,
    slash,
    sems,
):
    pairs = (
        (table_in, table),
        (lengths_in, lengths),
        (vertical_in, vertical),
        (slash_in, slash),
        (queries_in, queries),
    )
    copies = []
    for index, (source, target) in enumerate(pairs):
        copies.append(pltpu.make_async_copy(source, target, sems.at[index]))
        copies[-1].start()
    head = lax.axis_index("head")
    plane = lax.axis_index("ctx") * 2 + lax.axis_index("pool")
    first_row = plane * 64
    lane8 = lax.broadcasted_iota(jnp.int32, (8, 128), 1)
    lane = lax.broadcasted_iota(jnp.int32, (64, 128), 1)
    row = lax.broadcasted_iota(jnp.int32, (64, 128), 0)
    causal = jnp.where(lane - 64 <= row, 0.0, hide)
    hidden = jnp.where((lane == 0) | (lane == 32), 1.0, 0.0)
    own_heads = lax.broadcasted_iota(jnp.int32, (8, 32), 0) + head * 8
    pick = (own_heads == lax.broadcasted_iota(jnp.int32, (8, 32), 1)).astype(jnp.float32)
    for page in range(8):
        diagonal = (lane - 64 == row) & (plane == page)
        tag = diagonal | (((lane == 0) | (lane == 32)) & (plane < page))
        start = 4096 + page * 64
        key_tags[start : start + 64, :] = jnp.where(tag, 1.0, 0.0).astype(jnp.bfloat16)
    for copy in copies:
        copy.wait()
    for index in range(64):
        meta[table[index]] = index * 64
    for prompt in range(2):
        meta[64 + prompt] = lengths[prompt]

    def own(entries):
        picked = lax.dot_general(
            pick,
            entries[...].astype(jnp.float32),
            (((1,), (1,)), ((), ())),
            preferred_element_type=jnp.float32,
        )
        return (picked + 0.5).astype(jnp.int32)

    vert_rows, slash_rows = own(vertical), own(slash)
    page8 = lane8 % 32
    vert_hit = lane8 < 0
    for entry in range(16):
        vert_hit = vert_hit | (vert_rows[:, entry : entry + 1] == page8)
    for prompt in range(2):
        length = lengths[prompt]
        base_page = (length + first_row) // 64
        cut = (base_page + 1) * 64 - length - first_row
        tables = []
        for step in range(2):
            hit = vert_hit
            distance = base_page + step - page8
            for entry in range(16):
                hit = hit | (slash_rows[:, entry : entry + 1] == distance)
            shown = hit & (page8 * 64 < length) & (lane8 // 32 == prompt)
            tables.append(jnp.where(shown, 0.0, hide))
        for group in range(8):
            rows = slice(group * 64, (group + 1) * 64)
            bias = jnp.where(
                row < cut, tables[0][group : group + 1, :], tables[1][group : group + 1, :]
            )
            bias = jnp.where(lane < 64, bias, causal)
            wide_queries[prompt, rows, :128] = queries[prompt, :, group * 128 : (group + 1) * 128]
            wide_queries[prompt, rows, 128:] = bias.astype(jnp.bfloat16)
        for page in range(32):
            tag = jnp.where(lane[:16] == prompt * 32 + page, 1.0, 0.0)
            tag = jnp.where(page * 64 < length, tag, hidden[:16]).astype(jnp.bfloat16)
            start = prompt * 2048 + page * 64
            key_tags[start : start + 64, :] = jnp.concatenate([tag] * 4, axis=0)
        page = jnp.minimum(length // 64, 31)
        tag = jnp.where(lane == prompt * 32 + page, 1.0, 0.0)
        tag = jnp.where(row + page * 64 < length, tag, hidden).astype(jnp.bfloat16)
        key_tags[pl.ds(pl.multiple_of(prompt * 2048 + page * 64, 64), 64), :] = tag


def mask(lengths, table, queries, vertical, slash):
    return pl.pallas_call(
        mask_kernel,
        out_shape=(
            pltpu.VMEM((2, 512, 256), jnp.bfloat16),
            pltpu.VMEM((4608, 128), jnp.bfloat16),
            pltpu.SMEM((72,), jnp.int32),
        ),
        in_specs=[pl.BlockSpec(memory_space=pltpu.HBM)] * 5,
        out_specs=[vmem] * 2 + [smem],
        scratch_shapes=[
            pltpu.SMEM((2,), jnp.int32),
            pltpu.SMEM((64,), jnp.int32),
            pltpu.VMEM((2, 64, 1024), jnp.bfloat16),
            pltpu.VMEM((16, 32), jnp.int32),
            pltpu.VMEM((16, 32), jnp.int32),
            pltpu.SemaphoreType.DMA((5,)),
        ],
        cost_estimate=pl.CostEstimate(
            flops=mask_flops, bytes_accessed=1000, transcendentals=0
        ),
        name="mask",
    )(lengths, table, queries, vertical, slash)


def origin(other, role):
    from_pool = lax.axis_index("pool") ^ other
    return lax.axis_index("ctx") ^ (0, 1 + from_pool, 2 - from_pool, 3)[role], from_pool


def tags_at(meta, key_tags, slot):
    return key_tags[pl.ds(pl.multiple_of(meta[slot], 64), 64), :]


def bundle_pages(meta, key_tags, bundle, other, role):
    from_ctx, from_pool = origin(other, role)
    pages = []
    slot = ((from_ctx * 4 + lax.axis_index("head")) * 2 + from_pool) * 2
    for within in range(2):
        tags = tags_at(meta, key_tags, slot + within)
        pages.append((bundle[2, within], tags, bundle[3, within]))
    return pages


def bundle_stretch(key_tags, bundle, other, role, prompt):
    from_ctx, from_pool = origin(other, role)
    start = pl.multiple_of(4096 + (from_ctx * 2 + from_pool) * 64, 64)
    return [(bundle[0, prompt], key_tags[pl.ds(start, 64), :], bundle[1, prompt])]


def joined_pages(meta, key_tags, pieces, other, role):
    from_ctx, from_pool = origin(other, role)
    pages = []
    for shift in range(1, 4):
        slot = ((from_ctx * 4 + (lax.axis_index("head") ^ shift)) * 2 + from_pool) * 2
        for within in range(2):
            place = slice((shift - 1) * 128 + within * 64, (shift - 1) * 128 + within * 64 + 64)
            tags = tags_at(meta, key_tags, slot + within)
            pages.append((pieces[0, place, :], tags, pieces[1, place, :]))
    return pages


def stack(pages):
    keys = jnp.concatenate([page[0] for page in pages], axis=0)
    tags = jnp.concatenate([page[1] for page in pages], axis=0)
    values = jnp.concatenate([page[2] for page in pages], axis=0)
    ones = jnp.ones(values.shape, jnp.bfloat16)
    return jnp.concatenate([keys, tags], axis=1), jnp.concatenate([values, ones], axis=1)


def absorb_pages(wide_queries, shared, own, state, scores):
    shared_keys, shared_values = stack(shared)
    width = shared_keys.shape[0]
    own = [stack(pages) if pages else None for pages in own]
    highs, results = [], []
    for prompt in range(2):
        high = None
        for start, pair in ((0, (shared_keys,)), (width, own[prompt])):
            if pair is None:
                continue
            found = lax.dot_general(
                wide_queries[prompt],
                pair[0],
                (((1,), (1,)), ((), ())),
                preferred_element_type=jnp.float32,
            )
            scores[prompt, :, start : start + found.shape[1]] = found
            for column in range(0, found.shape[1], 128):
                part = found[:, column : column + 128]
                high = part if high is None else jnp.maximum(high, part)
        if state is not None:
            high = jnp.maximum(high, state[0][prompt])
        highs.append(jnp.max(high, axis=1, keepdims=True))
    for prompt in range(2):
        highest = highs[prompt]
        weights = jnp.exp2((scores[prompt] - highest) * scale).astype(jnp.bfloat16)
        sums = jnp.dot(
            weights[:, :width], shared_values, preferred_element_type=jnp.float32
        )
        if own[prompt] is not None:
            sums += jnp.dot(
                weights[:, width:], own[prompt][1], preferred_element_type=jnp.float32
            )
        numerator, totals = sums[:, :128], sums[:, 128:]
        if state is not None:
            factor = jnp.exp2((state[0][prompt] - highest) * scale)
            numerator = numerator + state[1][prompt, :, :128] * factor
            totals = totals + state[1][prompt, :, 128:] * factor
        results.append((highest, numerator, totals))
    return results


def keep(results, high_out, sums_out):
    for prompt, (highest, numerator, totals) in enumerate(results):
        high_out[prompt] = jnp.broadcast_to(highest, (512, 128))
        sums_out[prompt, :, :128] = numerator
        sums_out[prompt, :, 128:] = totals


def open_kernel(meta, wide_queries, key_tags, *rest):
    bundles, pieces = rest[:6], rest[6:8]
    high_out, sums_out, scores = rest[8:]
    shared, own = [], ([], [])
    for other in range(2):
        for role in range(3):
            bundle = bundles[other * 3 + role]
            shared += bundle_pages(meta, key_tags, bundle, other, role)
            for prompt in range(2):
                own[prompt].extend(bundle_stretch(key_tags, bundle, other, role, prompt))
        shared += joined_pages(meta, key_tags, pieces[other], other, 0)
    keep(absorb_pages(wide_queries, shared, own, None, scores), high_out, sums_out)


def middle_kernel(meta, wide_queries, key_tags, before, given, *rest):
    pieces = rest[:4]
    high_out, sums_out, scores = rest[4:]
    shared = []
    for other in range(2):
        for role in range(2):
            shared += joined_pages(meta, key_tags, pieces[other * 2 + role], other, 1 + role)
    state = (before, given)
    keep(absorb_pages(wide_queries, shared, ([], []), state, scores), high_out, sums_out)


def beside_kernel(meta, wide_queries, key_tags, before, given, *rest):
    bundles, mine = rest[:2], rest[2]
    high_out, sums_out, scores = rest[3:]
    shared, own = joined_pages(meta, key_tags, mine, 0, 3), ([], [])
    for other in range(2):
        shared += bundle_pages(meta, key_tags, bundles[other], other, 3)
        for prompt in range(2):
            own[prompt].extend(bundle_stretch(key_tags, bundles[other], other, 3, prompt))
    state = (before, given)
    keep(absorb_pages(wide_queries, shared, own, state, scores), high_out, sums_out)


def close_kernel(meta, wide_queries, key_tags, before, given, theirs, result, scores):
    shared = joined_pages(meta, key_tags, theirs, 1, 3)
    results = absorb_pages(wide_queries, shared, ([], []), (before, given), scores)
    for prompt, (_, numerator, totals) in enumerate(results):
        attended = (numerator / totals).astype(jnp.bfloat16)
        for group in range(8):
            rows = slice(group * 64, (group + 1) * 64)
            result[prompt, :, group * 128 : (group + 1) * 128] = attended[rows, :]


def call(kernel, name, out_shape, keys, *operands, flops=0):
    single = not isinstance(out_shape, tuple)
    return pl.pallas_call(
        kernel,
        out_shape=out_shape,
        in_specs=[smem] + [vmem] * (len(operands) - 1),
        out_specs=vmem if single else (vmem,) * len(out_shape),
        scratch_shapes=[pltpu.VMEM((2, 512, keys), jnp.float32)],
        compiler_params=pltpu.CompilerParams(vmem_limit_bytes=40 * 2**20),
        cost_estimate=pl.CostEstimate(flops=flops, bytes_accessed=1000, transcendentals=0),
        name=name,
    )(*operands)


def running():
    return (pltpu.VMEM((2, 512, 128), jnp.float32), pltpu.VMEM((2, 512, 256), jnp.float32))


def open_stage(meta, wide_queries, key_tags, bundles, pieces):
    return call(
        open_kernel, "open", running(), 30 * 64, meta, wide_queries, key_tags, *bundles, *pieces
    )


def middle_stage(meta, wide_queries, key_tags, state, pieces):
    return call(
        middle_kernel, "middle", running(), 24 * 64,
        meta, wide_queries, key_tags, *state, *pieces,
    )


def beside_stage(meta, wide_queries, key_tags, state, bundles, mine):
    return call(
        beside_kernel, "beside", running(), 12 * 64,
        meta, wide_queries, key_tags, *state, *bundles, mine, flops=beside_flops,
    )


def close_stage(meta, wide_queries, key_tags, state, theirs):
    return call(
        close_kernel, "close", jax.ShapeDtypeStruct((2, 64, 1024), jnp.bfloat16), 6 * 64,
        meta, wide_queries, key_tags, *state, theirs,
    )


def to_first(value):
    pairs = [(2 * c + p, 2 * (c ^ (1 + p)) + p) for c in range(4) for p in range(2)]
    return lax.ppermute(value, page_axes, pairs)


def to_second(value):
    pairs = [(2 * c + p, 2 * (c ^ (2 - p)) + p) for c in range(4) for p in range(2)]
    return lax.ppermute(value, page_axes, pairs)


def to_sibling(value):
    return lax.ppermute(value, "pool", [(0, 1), (1, 0)])


def small_body(
    queries,
    stretch_keys,
    stretch_values,
    slot_pool_keys,
    slot_pool_values,
    prefix_lengths,
    page_slot_table,
    vertical,
    slash,
):
    third, second, first, bundle = split(
        slot_pool_keys, slot_pool_values, stretch_keys, stretch_values
    )
    third, second, first = (
        lax.ppermute(piece, "head", [(z, z ^ shift) for z in range(4)])
        for shift, piece in ((3, third), (2, second), (1, first))
    )
    by_first, by_second = to_first(bundle), to_second(bundle)
    third, lengths = lax.optimization_barrier((third, prefix_lengths))
    masks = mask(lengths, page_slot_table, queries, vertical.T, slash.T)
    third, second, first, masks = lax.optimization_barrier((third, second, first, masks))
    joined = join(third, second, first)
    wide_queries, key_tags, meta = masks
    late_first, late_second = to_first(joined), to_second(joined)
    by_both = to_second(by_first)
    early = [bundle, by_first, by_second]
    early += [to_sibling(one) for one in early]
    state = open_stage(meta, wide_queries, key_tags, early, [joined, to_sibling(joined)])
    late_first, late_second, state = lax.optimization_barrier((late_first, late_second, state))
    late_both = to_second(late_first)
    late = [late_first, late_second]
    late += [to_sibling(one) for one in late]
    state = middle_stage(meta, wide_queries, key_tags, state, late)
    state, late_both = lax.optimization_barrier((state, late_both))
    far = [by_both, to_sibling(by_both)]
    theirs = to_sibling(late_both)
    state = beside_stage(meta, wide_queries, key_tags, state, far, late_both)
    return close_stage(meta, wide_queries, key_tags, state, theirs)


def solution(mesh):
    small = tuple(mesh.shape[axis] for axis in ("ctx", "head", "pool")) == (4, 4, 2)
    in_specs = (
        P(None, ("ctx", "pool"), "head"),
        P(None, ("ctx", "pool"), "head"),
        P(None, ("ctx", "pool"), "head"),
        P(("ctx", "head", "pool"), None, None),
        P(("ctx", "head", "pool"), None, None),
        P(),
        P(),
        P(),
        P(),
    )
    out_specs = P(None, ("ctx", "pool"), "head")
    return jax.shard_map(
        small_body if small else body,
        mesh=mesh,
        in_specs=in_specs,
        out_specs=out_specs,
        check_vma=False,
    )
```

```python
import math

import jax
import jax.numpy as jnp
from jax import lax
from jax.experimental import pallas as pl
from jax.experimental.pallas import tpu as pltpu
from jax.sharding import PartitionSpec as P

very_low = -1e30


def absorb(running, scores, allowed, values):
    highest, totals, numerator = running
    new_high = jnp.maximum(highest, jnp.max(jnp.where(allowed, scores, very_low), axis=-1))
    factor = jnp.exp(highest - new_high)
    weights = jnp.where(allowed, jnp.exp(scores - new_high[..., None]), 0.0)
    totals = totals * factor + jnp.sum(weights, axis=-1)
    numerator = numerator * factor[..., None] + jnp.einsum(
        "grk,kd->grd", weights.astype(jnp.bfloat16), values, preferred_element_type=jnp.float32
    )
    return (new_high, totals, numerator)


def body(
    queries,
    stretch_keys,
    stretch_values,
    slot_pool_keys,
    slot_pool_values,
    prefix_lengths,
    page_slot_table,
    vertical,
    slash,
):
    prompts, local_rows, row_width = queries.shape
    head_dim = stretch_keys.shape[2]
    group_size = row_width // head_dim
    page_len = slot_pool_keys.shape[1]
    owner_slots = slot_pool_keys.shape[0]
    slot_total = page_slot_table.shape[0]
    page_count = slot_total // prompts
    head_count = lax.axis_size("head")
    pool_count = lax.axis_size("pool")
    ctx_count = lax.axis_size("ctx")
    plane_size = ctx_count * pool_count
    ctx_index = lax.axis_index("ctx")
    pool_index = lax.axis_index("pool")
    head_index = lax.axis_index("head")
    plane_index = ctx_index * pool_count + pool_index
    stretch_len = plane_size * local_rows
    scaling = 1.0 / math.sqrt(head_dim)
    vert_rows = lax.dynamic_slice_in_dim(vertical, head_index * group_size, group_size, 0)
    slash_rows = lax.dynamic_slice_in_dim(slash, head_index * group_size, group_size, 0)
    page_ids = jnp.arange(page_count, dtype=jnp.int32)
    vert_hit = jnp.any(vert_rows[:, :, None] == page_ids[None, None, :], axis=1)
    row_ids = plane_index * local_rows + jnp.arange(local_rows, dtype=jnp.int32)
    page_keys, page_values = (
        lax.all_to_all(slot_pool_keys, "head", split_axis=2, concat_axis=0, tiled=True),
        lax.all_to_all(slot_pool_values, "head", split_axis=2, concat_axis=0, tiled=True),
    )
    held_slots = owner_slots * head_count
    empty_state = (
        jnp.full((group_size, local_rows), very_low, jnp.float32),
        jnp.zeros((group_size, local_rows), jnp.float32),
        jnp.zeros((group_size, local_rows, head_dim), jnp.float32),
    )
    plane_keys, plane_values = (
        lax.all_gather(page_keys, ("ctx", "pool"), axis=0, tiled=True),
        lax.all_gather(page_values, ("ctx", "pool"), axis=0, tiled=True),
    )
    owner_index = page_slot_table // owner_slots
    within = page_slot_table % owner_slots
    owner_pool = owner_index % pool_count
    owner_head = owner_index // pool_count % head_count
    owner_ctx = owner_index // (pool_count * head_count)
    location = (
        (owner_ctx * pool_count + owner_pool) * held_slots + owner_head * owner_slots + within
    )
    ordered_keys = jnp.take(plane_keys, location, axis=0).reshape(
        prompts, page_count * page_len, head_dim
    )
    ordered_values = jnp.take(plane_values, location, axis=0).reshape(
        prompts, page_count * page_len, head_dim
    )
    key_span = min(2048, page_count * page_len)
    states = []
    for prompt in range(prompts):
        prefix_len = prefix_lengths[prompt]
        query_page = (prefix_len + row_ids) // page_len
        query_block = queries[prompt].reshape(local_rows, group_size, head_dim)
        prompt_keys = ordered_keys[prompt]
        prompt_values = ordered_values[prompt]

        def prefix_step(block_index, running):
            first_key = block_index * key_span
            key_part = lax.dynamic_slice_in_dim(prompt_keys, first_key, key_span, 0)
            value_part = lax.dynamic_slice_in_dim(prompt_values, first_key, key_span, 0)
            key_ids = first_key + jnp.arange(key_span, dtype=jnp.int32)
            first_page = first_key // page_len
            page_part = lax.dynamic_slice_in_dim(vert_hit, first_page, key_span // page_len, 1)
            distance = (
                query_page[:, None]
                - (first_page + jnp.arange(key_span // page_len, dtype=jnp.int32))[None, :]
            )
            slash_hit = jnp.any(slash_rows[:, :, None, None] == distance[None, None], axis=1)
            chosen = page_part[:, None, :] | slash_hit
            allowed = jnp.repeat(chosen, page_len, axis=2) & (key_ids < prefix_len)[None, None, :]
            scores = (
                jnp.einsum("rgd,kd->grk", query_block, key_part, preferred_element_type=jnp.float32)
                * scaling
            )
            return absorb(running, scores, allowed, value_part)

        upper_bound = (prefix_len + key_span - 1) // key_span
        states.append(lax.fori_loop(0, upper_bound, prefix_step, empty_state))
    plane_stretch_keys, plane_stretch_values = (
        lax.all_gather(stretch_keys, ("ctx", "pool"), axis=1, tiled=True),
        lax.all_gather(stretch_values, ("ctx", "pool"), axis=1, tiled=True),
    )
    stretch_span = min(2048, stretch_len)
    outputs = []
    for prompt in range(prompts):
        query_block = queries[prompt].reshape(local_rows, group_size, head_dim)
        prompt_keys = plane_stretch_keys[prompt]
        prompt_values = plane_stretch_values[prompt]

        def stretch_step(block_index, running):
            first_key = block_index * stretch_span
            key_ids = first_key + jnp.arange(stretch_span, dtype=jnp.int32)
            allowed = jnp.broadcast_to(
                (key_ids[None, :] <= row_ids[:, None])[None], (group_size, local_rows, stretch_span)
            )
            scores = (
                jnp.einsum(
                    "rgd,kd->grk", query_block, prompt_keys, preferred_element_type=jnp.float32
                )
                * scaling
            )
            return absorb(running, scores, allowed, prompt_values)

        upper_bound = (plane_index * local_rows + local_rows - 1) // stretch_span + 1
        highest, totals, numerator = lax.fori_loop(0, upper_bound, stretch_step, states[prompt])
        result = numerator / totals[..., None]
        outputs.append(
            result.transpose(1, 0, 2).reshape(local_rows, row_width).astype(jnp.bfloat16)
        )
    return jnp.stack(outputs)


page_axes = ("ctx", "pool")
hide = -(2.0**126)
scale = 1.4426950408889634 / math.sqrt(128.0)
join_flops = 6 * 10**9
mask_flops = 0
beside_flops = 20 * 10**8
vmem = pl.BlockSpec(memory_space=pltpu.VMEM)
smem = pl.BlockSpec(memory_space=pltpu.SMEM)


def split_kernel(
    pool_keys, pool_values, stretch_keys, stretch_values, third, second, first, early, sems
):
    head = lax.axis_index("head")
    copies = []

    def add(source, target):
        copy = pltpu.make_async_copy(source, target, sems.at[len(copies)])
        copy.start()
        copies.append(copy)

    for shift, target in ((3, third), (2, second), (1, first), (0, None)):
        columns = pl.ds(pl.multiple_of((head ^ shift) * 128, 128), 128)
        for which, pool in enumerate((pool_keys, pool_values)):
            place = early.at[2 + which] if target is None else target.at[which]
            add(pool.at[:, :, columns], place)
    add(stretch_keys, early.at[0])
    add(stretch_values, early.at[1])
    for copy in copies:
        copy.wait()


def split(pool_keys, pool_values, stretch_keys, stretch_values):
    piece = pltpu.VMEM((2, 2, 64, 128), jnp.bfloat16)
    bundle = pltpu.VMEM((4, 2, 64, 128), jnp.bfloat16)
    return pl.pallas_call(
        split_kernel,
        out_shape=(piece, piece, piece, bundle),
        in_specs=[pl.BlockSpec(memory_space=pltpu.HBM)] * 4,
        out_specs=[vmem] * 4,
        scratch_shapes=[pltpu.SemaphoreType.DMA((10,))],
        name="split",
    )(pool_keys, pool_values, stretch_keys, stretch_values)


def join_kernel(third, second, first, joined):
    for index, piece in enumerate((first, second, third)):
        for which in range(2):
            for within in range(2):
                start = index * 128 + within * 64
                joined[which, start : start + 64, :] = piece[which, within]


def join(third, second, first):
    return pl.pallas_call(
        join_kernel,
        out_shape=pltpu.VMEM((2, 384, 128), jnp.bfloat16),
        in_specs=[vmem] * 3,
        out_specs=vmem,
        compiler_params=pltpu.CompilerParams(vmem_limit_bytes=4 * 2**20),
        cost_estimate=pl.CostEstimate(
            flops=join_flops, bytes_accessed=400000, transcendentals=0
        ),
        name="join",
    )(third, second, first)


def mask_kernel(
    lengths_in,
    table_in,
    queries_in,
    vertical_in,
    slash_in,
    wide_queries,
    key_tags,
    meta,
    lengths,
    table,
    queries,
    vertical,
    slash,
    sems,
):
    pairs = (
        (table_in, table),
        (lengths_in, lengths),
        (vertical_in, vertical),
        (slash_in, slash),
        (queries_in, queries),
    )
    copies = []
    for index, (source, target) in enumerate(pairs):
        copies.append(pltpu.make_async_copy(source, target, sems.at[index]))
        copies[-1].start()
    head = lax.axis_index("head")
    plane = lax.axis_index("ctx") * 2 + lax.axis_index("pool")
    first_row = plane * 64
    lane8 = lax.broadcasted_iota(jnp.int32, (8, 128), 1)
    lane = lax.broadcasted_iota(jnp.int32, (64, 128), 1)
    row = lax.broadcasted_iota(jnp.int32, (64, 128), 0)
    causal = jnp.where(lane - 64 <= row, 0.0, hide)
    hidden = jnp.where((lane == 0) | (lane == 32), 1.0, 0.0)
    own_heads = lax.broadcasted_iota(jnp.int32, (8, 32), 0) + head * 8
    pick = (own_heads == lax.broadcasted_iota(jnp.int32, (8, 32), 1)).astype(jnp.float32)
    for page in range(8):
        diagonal = (lane - 64 == row) & (plane == page)
        tag = diagonal | (((lane == 0) | (lane == 32)) & (plane < page))
        start = 4096 + page * 64
        key_tags[start : start + 64, :] = jnp.where(tag, 1.0, 0.0).astype(jnp.bfloat16)
    for copy in copies:
        copy.wait()
    for index in range(64):
        meta[table[index]] = index * 64
    for prompt in range(2):
        meta[64 + prompt] = lengths[prompt]

    def own(entries):
        picked = lax.dot_general(
            pick,
            entries[...].astype(jnp.float32),
            (((1,), (1,)), ((), ())),
            preferred_element_type=jnp.float32,
        )
        return (picked + 0.5).astype(jnp.int32)

    vert_rows, slash_rows = own(vertical), own(slash)
    page8 = lane8 % 32
    vert_hit = lane8 < 0
    for entry in range(16):
        vert_hit = vert_hit | (vert_rows[:, entry : entry + 1] == page8)
    for prompt in range(2):
        length = lengths[prompt]
        base_page = (length + first_row) // 64
        cut = (base_page + 1) * 64 - length - first_row
        tables = []
        for step in range(2):
            hit = vert_hit
            distance = base_page + step - page8
            for entry in range(16):
                hit = hit | (slash_rows[:, entry : entry + 1] == distance)
            shown = hit & (page8 * 64 < length) & (lane8 // 32 == prompt)
            tables.append(jnp.where(shown, 0.0, hide))
        for group in range(8):
            rows = slice(group * 64, (group + 1) * 64)
            bias = jnp.where(
                row < cut, tables[0][group : group + 1, :], tables[1][group : group + 1, :]
            )
            bias = jnp.where(lane < 64, bias, causal)
            wide_queries[prompt, rows, :128] = queries[prompt, :, group * 128 : (group + 1) * 128]
            wide_queries[prompt, rows, 128:] = bias.astype(jnp.bfloat16)
        for page in range(32):
            tag = jnp.where(lane[:16] == prompt * 32 + page, 1.0, 0.0)
            tag = jnp.where(page * 64 < length, tag, hidden[:16]).astype(jnp.bfloat16)
            start = prompt * 2048 + page * 64
            key_tags[start : start + 64, :] = jnp.concatenate([tag] * 4, axis=0)
        page = jnp.minimum(length // 64, 31)
        tag = jnp.where(lane == prompt * 32 + page, 1.0, 0.0)
        tag = jnp.where(row + page * 64 < length, tag, hidden).astype(jnp.bfloat16)
        key_tags[pl.ds(pl.multiple_of(prompt * 2048 + page * 64, 64), 64), :] = tag


def mask(lengths, table, queries, vertical, slash):
    return pl.pallas_call(
        mask_kernel,
        out_shape=(
            pltpu.VMEM((2, 512, 256), jnp.bfloat16),
            pltpu.VMEM((4608, 128), jnp.bfloat16),
            pltpu.SMEM((72,), jnp.int32),
        ),
        in_specs=[pl.BlockSpec(memory_space=pltpu.HBM)] * 5,
        out_specs=[vmem] * 2 + [smem],
        scratch_shapes=[
            pltpu.SMEM((2,), jnp.int32),
            pltpu.SMEM((64,), jnp.int32),
            pltpu.VMEM((2, 64, 1024), jnp.bfloat16),
            pltpu.VMEM((16, 32), jnp.int32),
            pltpu.VMEM((16, 32), jnp.int32),
            pltpu.SemaphoreType.DMA((5,)),
        ],
        cost_estimate=pl.CostEstimate(
            flops=mask_flops, bytes_accessed=1000, transcendentals=0
        ),
        name="mask",
    )(lengths, table, queries, vertical, slash)


def origin(other, role):
    from_pool = lax.axis_index("pool") ^ other
    return lax.axis_index("ctx") ^ (0, 1 + from_pool, 2 - from_pool, 3)[role], from_pool


def tags_at(meta, key_tags, slot):
    return key_tags[pl.ds(pl.multiple_of(meta[slot], 64), 64), :]


def bundle_pages(meta, key_tags, bundle, other, role):
    from_ctx, from_pool = origin(other, role)
    pages = []
    slot = ((from_ctx * 4 + lax.axis_index("head")) * 2 + from_pool) * 2
    for within in range(2):
        tags = tags_at(meta, key_tags, slot + within)
        pages.append((bundle[2, within], tags, bundle[3, within]))
    return pages


def bundle_stretch(key_tags, bundle, other, role, prompt):
    from_ctx, from_pool = origin(other, role)
    start = pl.multiple_of(4096 + (from_ctx * 2 + from_pool) * 64, 64)
    return [(bundle[0, prompt], key_tags[pl.ds(start, 64), :], bundle[1, prompt])]


def joined_pages(meta, key_tags, pieces, other, role):
    from_ctx, from_pool = origin(other, role)
    pages = []
    for shift in range(1, 4):
        slot = ((from_ctx * 4 + (lax.axis_index("head") ^ shift)) * 2 + from_pool) * 2
        for within in range(2):
            place = slice((shift - 1) * 128 + within * 64, (shift - 1) * 128 + within * 64 + 64)
            tags = tags_at(meta, key_tags, slot + within)
            pages.append((pieces[0, place, :], tags, pieces[1, place, :]))
    return pages


def stack(pages):
    keys = jnp.concatenate([page[0] for page in pages], axis=0)
    tags = jnp.concatenate([page[1] for page in pages], axis=0)
    values = jnp.concatenate([page[2] for page in pages], axis=0)
    ones = jnp.ones(values.shape, jnp.bfloat16)
    return jnp.concatenate([keys, tags], axis=1), jnp.concatenate([values, ones], axis=1)


def absorb_pages(wide_queries, shared, own, state, scores):
    shared_keys, shared_values = stack(shared)
    width = shared_keys.shape[0]
    own = [stack(pages) if pages else None for pages in own]
    highs, results = [], []
    for prompt in range(2):
        high = None
        for start, pair in ((0, (shared_keys,)), (width, own[prompt])):
            if pair is None:
                continue
            found = lax.dot_general(
                wide_queries[prompt],
                pair[0],
                (((1,), (1,)), ((), ())),
                preferred_element_type=jnp.float32,
            )
            scores[prompt, :, start : start + found.shape[1]] = found
            for column in range(0, found.shape[1], 128):
                part = found[:, column : column + 128]
                high = part if high is None else jnp.maximum(high, part)
        if state is not None:
            high = jnp.maximum(high, state[0][prompt])
        highs.append(jnp.max(high, axis=1, keepdims=True))
    for prompt in range(2):
        highest = highs[prompt]
        weights = jnp.exp2((scores[prompt] - highest) * scale).astype(jnp.bfloat16)
        sums = jnp.dot(
            weights[:, :width], shared_values, preferred_element_type=jnp.float32
        )
        if own[prompt] is not None:
            sums += jnp.dot(
                weights[:, width:], own[prompt][1], preferred_element_type=jnp.float32
            )
        numerator, totals = sums[:, :128], sums[:, 128:]
        if state is not None:
            factor = jnp.exp2((state[0][prompt] - highest) * scale)
            numerator = numerator + state[1][prompt, :, :128] * factor
            totals = totals + state[1][prompt, :, 128:] * factor
        results.append((highest, numerator, totals))
    return results


def keep(results, high_out, sums_out):
    for prompt, (highest, numerator, totals) in enumerate(results):
        high_out[prompt] = jnp.broadcast_to(highest, (512, 128))
        sums_out[prompt, :, :128] = numerator
        sums_out[prompt, :, 128:] = totals


def open_kernel(meta, wide_queries, key_tags, *rest):
    bundles, pieces = rest[:6], rest[6:8]
    high_out, sums_out, scores = rest[8:]
    shared, own = [], ([], [])
    for other in range(2):
        for role in range(3):
            bundle = bundles[other * 3 + role]
            shared += bundle_pages(meta, key_tags, bundle, other, role)
            for prompt in range(2):
                own[prompt].extend(bundle_stretch(key_tags, bundle, other, role, prompt))
        shared += joined_pages(meta, key_tags, pieces[other], other, 0)
    keep(absorb_pages(wide_queries, shared, own, None, scores), high_out, sums_out)


def middle_kernel(meta, wide_queries, key_tags, before, given, *rest):
    bundle, pieces = rest[0], rest[1:5]
    high_out, sums_out, scores = rest[5:]
    shared = bundle_pages(meta, key_tags, bundle, 0, 3)
    for other in range(2):
        for role in range(2):
            shared += joined_pages(meta, key_tags, pieces[other * 2 + role], other, 1 + role)
    state = (before, given)
    keep(absorb_pages(wide_queries, shared, ([], []), state, scores), high_out, sums_out)


def beside_kernel(meta, wide_queries, key_tags, before, given, *rest):
    bundles, mine = rest[:2], rest[2]
    high_out, sums_out, scores = rest[3:]
    shared, own = joined_pages(meta, key_tags, mine, 0, 3), ([], [])
    for other in range(2):
        for prompt in range(2):
            own[prompt].extend(bundle_stretch(key_tags, bundles[other], other, 3, prompt))
    shared += bundle_pages(meta, key_tags, bundles[1], 1, 3)
    state = (before, given)
    keep(absorb_pages(wide_queries, shared, own, state, scores), high_out, sums_out)


def close_kernel(meta, wide_queries, key_tags, before, given, theirs, result, scores):
    shared = joined_pages(meta, key_tags, theirs, 1, 3)
    results = absorb_pages(wide_queries, shared, ([], []), (before, given), scores)
    for prompt, (_, numerator, totals) in enumerate(results):
        attended = (numerator / totals).astype(jnp.bfloat16)
        for group in range(8):
            rows = slice(group * 64, (group + 1) * 64)
            result[prompt, :, group * 128 : (group + 1) * 128] = attended[rows, :]


def call(kernel, name, out_shape, keys, *operands, flops=0):
    single = not isinstance(out_shape, tuple)
    return pl.pallas_call(
        kernel,
        out_shape=out_shape,
        in_specs=[smem] + [vmem] * (len(operands) - 1),
        out_specs=vmem if single else (vmem,) * len(out_shape),
        scratch_shapes=[pltpu.VMEM((2, 512, keys), jnp.float32)],
        compiler_params=pltpu.CompilerParams(vmem_limit_bytes=40 * 2**20),
        cost_estimate=pl.CostEstimate(flops=flops, bytes_accessed=1000, transcendentals=0),
        name=name,
    )(*operands)


def running():
    return (pltpu.VMEM((2, 512, 128), jnp.float32), pltpu.VMEM((2, 512, 256), jnp.float32))


def open_stage(meta, wide_queries, key_tags, bundles, pieces):
    return call(
        open_kernel, "open", running(), 30 * 64, meta, wide_queries, key_tags, *bundles, *pieces
    )


def middle_stage(meta, wide_queries, key_tags, state, bundle, pieces):
    return call(
        middle_kernel, "middle", running(), 26 * 64,
        meta, wide_queries, key_tags, *state, bundle, *pieces,
    )


def beside_stage(meta, wide_queries, key_tags, state, bundles, mine):
    return call(
        beside_kernel, "beside", running(), 10 * 64,
        meta, wide_queries, key_tags, *state, *bundles, mine, flops=beside_flops,
    )


def close_stage(meta, wide_queries, key_tags, state, theirs):
    return call(
        close_kernel, "close", jax.ShapeDtypeStruct((2, 64, 1024), jnp.bfloat16), 6 * 64,
        meta, wide_queries, key_tags, *state, theirs,
    )


def to_first(value):
    pairs = [(2 * c + p, 2 * (c ^ (1 + p)) + p) for c in range(4) for p in range(2)]
    return lax.ppermute(value, page_axes, pairs)


def to_second(value):
    pairs = [(2 * c + p, 2 * (c ^ (2 - p)) + p) for c in range(4) for p in range(2)]
    return lax.ppermute(value, page_axes, pairs)


def to_sibling(value):
    return lax.ppermute(value, "pool", [(0, 1), (1, 0)])


def small_body(
    queries,
    stretch_keys,
    stretch_values,
    slot_pool_keys,
    slot_pool_values,
    prefix_lengths,
    page_slot_table,
    vertical,
    slash,
):
    third, second, first, bundle = split(
        slot_pool_keys, slot_pool_values, stretch_keys, stretch_values
    )
    third, second, first = (
        lax.ppermute(piece, "head", [(z, z ^ shift) for z in range(4)])
        for shift, piece in ((3, third), (2, second), (1, first))
    )
    by_first, by_second = to_first(bundle), to_second(bundle)
    third, lengths = lax.optimization_barrier((third, prefix_lengths))
    masks = mask(lengths, page_slot_table, queries, vertical.T, slash.T)
    third, second, first, masks = lax.optimization_barrier((third, second, first, masks))
    joined = join(third, second, first)
    wide_queries, key_tags, meta = masks
    late_first, late_second = to_first(joined), to_second(joined)
    by_both = to_second(by_first)
    early = [bundle, by_first, by_second]
    early += [to_sibling(one) for one in early]
    state = open_stage(meta, wide_queries, key_tags, early, [joined, to_sibling(joined)])
    late_first, late_second, state = lax.optimization_barrier((late_first, late_second, state))
    late_both = to_second(late_first)
    late = [late_first, late_second]
    late += [to_sibling(one) for one in late]
    state = middle_stage(meta, wide_queries, key_tags, state, by_both, late)
    state, late_both = lax.optimization_barrier((state, late_both))
    far = [by_both, to_sibling(by_both)]
    theirs = to_sibling(late_both)
    state = beside_stage(meta, wide_queries, key_tags, state, far, late_both)
    return close_stage(meta, wide_queries, key_tags, state, theirs)


def solution(mesh):
    small = tuple(mesh.shape[axis] for axis in ("ctx", "head", "pool")) == (4, 4, 2)
    in_specs = (
        P(None, ("ctx", "pool"), "head"),
        P(None, ("ctx", "pool"), "head"),
        P(None, ("ctx", "pool"), "head"),
        P(("ctx", "head", "pool"), None, None),
        P(("ctx", "head", "pool"), None, None),
        P(),
        P(),
        P(),
        P(),
    )
    out_specs = P(None, ("ctx", "pool"), "head")
    return jax.shard_map(
        small_body if small else body,
        mesh=mesh,
        in_specs=in_specs,
        out_specs=out_specs,
        check_vma=False,
    )
```
